32 devices in a mesh: wide: 16 (over z, y, x), narrow: 2 (over core).
Axes of the slice: x: 2, y: 2, z: 4, core: 2. Of those that a mesh axis runs over, the one named last changes fastest.
Arguments:
- inputs: bfloat16 [16, 1024, 768], P('wide', 'narrow'), may hold values from -6 to 6
- enc_norm_gain: bfloat16 [768], P(('wide', 'narrow')), may hold values from 0.25 to 1.75
- enc_norm_bias: bfloat16 [768], P(('wide', 'narrow')), may hold values from -3 to 3
- enc_qkv: bfloat16 [768, 2304], P(('wide', 'narrow')), may hold values from -0.21875 to 0.21875
- enc_proj: bfloat16 [768, 768], P(('wide', 'narrow')), may hold values from -1.75 to 1.75
- enc_mlp_gain: bfloat16 [768], P(('wide', 'narrow')), may hold values from 0.25 to 1.75
- enc_mlp_bias: bfloat16 [768], P(('wide', 'narrow')), may hold values from -3 to 3
- enc_up: bfloat16 [768, 3072], P(('wide', 'narrow')), may hold values from -0.21875 to 0.21875
- enc_down: bfloat16 [3072, 768], P(('wide', 'narrow')), may hold values from -0.109375 to 0.109375
- embed_weight: bfloat16 [768, 512], P(('wide', 'narrow')), may hold values from -0.21875 to 0.21875
- mask_token: bfloat16 [512], P(('wide', 'narrow')), may hold values from -4 to 4
- dec_norm_gain: bfloat16 [512], P(('wide', 'narrow')), may hold values from 0.25 to 1.75
- dec_norm_bias: bfloat16 [512], P(('wide', 'narrow')), may hold values from -3 to 3
- dec_qkv: bfloat16 [512, 1536], P(('wide', 'narrow')), may hold values from -0.25 to 0.25
- dec_proj: bfloat16 [512, 512], P(('wide', 'narrow')), may hold values from -4 to 4
- dec_mlp_gain: bfloat16 [512], P(('wide', 'narrow')), may hold values from 0.25 to 1.75
- dec_mlp_bias: bfloat16 [512], P(('wide', 'narrow')), may hold values from -3 to 3
- dec_up: bfloat16 [512, 2048], P(('wide', 'narrow')), may hold values from -0.25 to 0.25
- dec_down: bfloat16 [2048, 512], P(('wide', 'narrow')), may hold values from -0.125 to 0.125
- cotangent: bfloat16 [256, 196, 512], P(('wide', 'narrow')), may hold values from -6 to 6
- visible_counts: int32 [16, 16], P('wide'), may hold values from 1 to 128, as said below
- patch_positions: int32 [16, 1024], P('wide', 'narrow'), may hold values from 0 to 195, as said below
- image_owner: int32 [256], replicated, may hold values from 0 to 255, as said below
Outputs:
- decoded: bfloat16 [256, 196, 512], P(('wide', 'narrow'))
- grad_inputs: float32 [16, 1024, 768], P('wide', 'narrow')
- grad_enc_norm_gain: float32 [768], P(('wide', 'narrow'))
- grad_enc_norm_bias: float32 [768], P(('wide', 'narrow'))
- grad_enc_qkv: float32 [768, 2304], P(('wide', 'narrow'))
- grad_enc_proj: float32 [768, 768], P(('wide', 'narrow'))
- grad_enc_mlp_gain: float32 [768], P(('wide', 'narrow'))
- grad_enc_mlp_bias: float32 [768], P(('wide', 'narrow'))
- grad_enc_up: float32 [768, 3072], P(('wide', 'narrow'))
- grad_enc_down: float32 [3072, 768], P(('wide', 'narrow'))
- grad_embed_weight: float32 [768, 512], P(('wide', 'narrow'))
- grad_mask_token: float32 [512], P(('wide', 'narrow'))
- grad_dec_norm_gain: float32 [512], P(('wide', 'narrow'))
- grad_dec_norm_bias: float32 [512], P(('wide', 'narrow'))
- grad_dec_qkv: float32 [512, 1536], P(('wide', 'narrow'))
- grad_dec_proj: float32 [512, 512], P(('wide', 'narrow'))
- grad_dec_mlp_gain: float32 [512], P(('wide', 'narrow'))
- grad_dec_mlp_bias: float32 [512], P(('wide', 'narrow'))
- grad_dec_up: float32 [512, 2048], P(('wide', 'narrow'))
- grad_dec_down: float32 [2048, 512], P(('wide', 'narrow'))
The draws below stay inside these ranges and needn't reach their ends.
Inputs may be any that keep to these rules, and one draw needn't show every extreme that they name: `visible_counts`: each row sums to 1024. In each row exactly one image has 128 visible patches, and it is the first or the last image of its sequence. `patch_positions`: the positions of the rows of one image are distinct. A permutation of the images: image i is decoded on device image_owner[i] // 8 of wide+narrow (wide index times 2 plus narrow index), in slot image_owner[i] % 8. The images of the sequence of wide index w are decoded by the two devices of wide index w, 8 on each.
All inputs are finite; a program needn't handle non-finite values.
Results may differ from the reference program's by a relative error of at most 0.017.
Values may be sent and summed in bfloat16 or wider, within the bound.
No kernel may reach another device: no remote copies, remote signals or barrier semaphores. Data moves between devices by JAX's collectives and lax.ppermute only.
A program may use at most 384 MiB of HBM per device.

```python
import math
import jax
import jax.numpy as jnp
from jax import lax

D = 768
HEADS = 12
HEAD_DIM = 64
FF = 3072
DD = 512
DHEADS = 16
DHEAD_DIM = 32
DFF = 2048
PATCHES = 196
AVG = 64
SEQ = 1024
SEQS = 16
IMG_SEQ = 16
IMAGES = 256
N_WIDE = 16


def sequence_counts(key):
    average = SEQ // IMG_SEQ
    half_step = average // 2
    key_side, key_rest = jax.random.split(jax.random.fold_in(key, 11))
    shifts = jax.random.randint(key_rest, (SEQS, IMG_SEQ), 1 - half_step, half_step)
    at_end = jax.random.randint(key_side, (SEQS, 1), 0, 2)
    column = jnp.arange(IMG_SEQ)[None, :]
    largest = at_end * (IMG_SEQ - 1)
    follower = (largest + 1) % IMG_SEQ
    shifts = jnp.where(column == largest, half_step, shifts)
    shifts = jnp.where(column == follower, -half_step, shifts)
    return (average + shifts - jnp.roll(shifts, -1, axis=1)).astype(jnp.int32)


def draw_visible_counts(key, part):
    return sequence_counts(key)


def draw_patch_positions(key, part):
    counts = sequence_counts(key)
    key = jax.random.fold_in(key, 3)
    image_ends = jnp.cumsum(counts, axis=1)
    position = jnp.arange(SEQ)
    segment_ids = jnp.sum((image_ends[:, None, :] <= position[None, :, None]).astype(jnp.int32), axis=2)
    starts = image_ends - counts
    row_start = jnp.take_along_axis(starts, segment_ids, axis=1)
    row_rank = position[None, :] - row_start
    orders = jax.vmap(lambda subkey: jax.random.permutation(subkey, PATCHES))(jax.random.split(key, SEQS * IMG_SEQ))
    flat_index = (jnp.arange(SEQS)[:, None] * IMG_SEQ + segment_ids) * PATCHES + row_rank
    return orders.reshape(-1)[flat_index].astype(jnp.int32)


def draw_image_owner(key, part):
    key = jax.random.fold_in(key, 7)
    orders = jax.vmap(lambda subkey: jax.random.permutation(subkey, IMG_SEQ))(jax.random.split(key, SEQS))
    return (jnp.arange(SEQS)[:, None] * IMG_SEQ + orders).reshape(-1).astype(jnp.int32)


def shard_levels(rng, shape, shards, low, top_value):
    level, own = 1.0, jax.random.fold_in(rng, 6)
    for axis_at, parts in shards:
        draws = jnp.exp(jax.random.uniform(jax.random.fold_in(own, axis_at), (parts,), jnp.float32, low / len(shards), top_value / len(shards)))
        level = level * jnp.repeat(draws, shape[axis_at] // parts).reshape([-1 if axis == axis_at else 1 for axis in range(len(shape))])
    return level


def noise(own_key, dims, scale, most, shards=(), dtype=jnp.bfloat16):
    result = scale * jax.random.normal(own_key, dims, jnp.float32)
    if shards:
        result = result * shard_levels(own_key, dims, shards, -0.22, 0.18)
    return jnp.clip(result, -most, most).astype(dtype)


def setup_inputs(seed: int = 0) -> dict:
    seeds = jax.random.split(jax.random.key(seed), 24)
    inputs = noise(seeds[0], (SEQS, SEQ, D), 1.0, 6.0, ((0, 16), (1, 2)))
    enc_norm_gain = jnp.clip(1.0 + 0.15 * jax.random.normal(seeds[1], (D,), jnp.float32), 0.25, 1.75).astype(jnp.bfloat16)
    enc_norm_bias = noise(seeds[2], (D,), 0.3, 3.0, ((0, 32),))
    enc_qkv = noise(seeds[3], (D, 3 * D), D ** -0.5, 0.21875, ((0, 32),))
    enc_proj = noise(seeds[4], (D, D), (D // AVG) ** -0.5, 1.75, ((0, 32),))
    enc_mlp_gain = jnp.clip(1.0 + 0.15 * jax.random.normal(seeds[5], (D,), jnp.float32), 0.25, 1.75).astype(jnp.bfloat16)
    enc_mlp_bias = noise(seeds[6], (D,), 0.3, 3.0, ((0, 32),))
    enc_up = noise(seeds[7], (D, FF), D ** -0.5, 0.21875, ((0, 32),))
    enc_down = noise(seeds[8], (FF, D), FF ** -0.5, 0.109375, ((0, 32),))
    embed_weight = noise(seeds[9], (D, DD), D ** -0.5, 0.21875, ((0, 32),))
    mask_token = noise(seeds[10], (DD,), 1.0, 4.0, ((0, 32),))
    dec_norm_gain = jnp.clip(1.0 + 0.15 * jax.random.normal(seeds[11], (DD,), jnp.float32), 0.25, 1.75).astype(jnp.bfloat16)
    dec_norm_bias = noise(seeds[12], (DD,), 0.3, 3.0, ((0, 32),))
    dec_qkv = noise(seeds[13], (DD, 3 * DD), DD ** -0.5, 0.25, ((0, 32),))
    dec_proj = noise(seeds[14], (DD, DD), (max(DD // PATCHES, 1)) ** -0.5, 4.0, ((0, 32),))
    dec_mlp_gain = jnp.clip(1.0 + 0.15 * jax.random.normal(seeds[15], (DD,), jnp.float32), 0.25, 1.75).astype(jnp.bfloat16)
    dec_mlp_bias = noise(seeds[16], (DD,), 0.3, 3.0, ((0, 32),))
    dec_up = noise(seeds[17], (DD, DFF), DD ** -0.5, 0.25, ((0, 32),))
    dec_down = noise(seeds[18], (DFF, DD), DFF ** -0.5, 0.125, ((0, 32),))
    cotangent = noise(seeds[19], (IMAGES, PATCHES, DD), 1.0, 6.0, ((0, 32),))
    visible_counts = draw_visible_counts(jax.random.fold_in(seeds[23], 71), 0)
    patch_positions = draw_patch_positions(jax.random.fold_in(seeds[23], 71), 0)
    image_owner = draw_image_owner(jax.random.fold_in(seeds[23], 71), 0)
    return dict(inputs=inputs, enc_norm_gain=enc_norm_gain, enc_norm_bias=enc_norm_bias, enc_qkv=enc_qkv, enc_proj=enc_proj, enc_mlp_gain=enc_mlp_gain, enc_mlp_bias=enc_mlp_bias, enc_up=enc_up, enc_down=enc_down, embed_weight=embed_weight, mask_token=mask_token, dec_norm_gain=dec_norm_gain, dec_norm_bias=dec_norm_bias, dec_qkv=dec_qkv, dec_proj=dec_proj, dec_mlp_gain=dec_mlp_gain, dec_mlp_bias=dec_mlp_bias, dec_up=dec_up, dec_down=dec_down, cotangent=cotangent, visible_counts=visible_counts, patch_positions=patch_positions, image_owner=image_owner)


@jax.custom_vjp
def low(v):
    return lax.optimization_barrier(v.astype(jnp.bfloat16)).astype(jnp.float32)

@jax.custom_vjp
def low_back(v):
    return v

def low_keep(v):
    return (low(v), None)

def low_pass(kept, grad):
    return (grad,)

def back_keep(v):
    return (v, None)

def back_low(kept, grad):
    return (low(grad),)
low.defvjp(low_keep, low_pass)
low_back.defvjp(back_keep, back_low)
EPSILON = 1e-06
NEGATIVE = -1e+30
HIGH = lax.Precision.HIGHEST

def product(left_side, right_side):
    return jnp.dot(left_side, right_side, precision=HIGH, preferred_element_type=jnp.float32)

def norm_rows(values, norm_gain, norm_bias):
    center = values - lax.optimization_barrier(jnp.mean(values, axis=-1, keepdims=True))
    scaled = center * lax.rsqrt(lax.optimization_barrier(jnp.mean(center * center, axis=-1, keepdims=True)) + EPSILON)
    return scaled * norm_gain + norm_bias

def position_table(model_width):
    grid_side = math.isqrt(PATCHES)
    patch_index = jnp.arange(PATCHES).astype(jnp.int32)
    row_coord = (patch_index // grid_side).astype(jnp.float32)[:, None]
    col_coord = (patch_index % grid_side).astype(jnp.float32)[:, None]
    quarter = model_width // 4
    frequency = jnp.power(10000.0, -jnp.arange(quarter).astype(jnp.float32) / quarter)[None, :]
    return jnp.concatenate([jnp.sin(row_coord * frequency), jnp.cos(row_coord * frequency), jnp.sin(col_coord * frequency), jnp.cos(col_coord * frequency)], axis=1)

def attention_core(queries, keys_all, values_all, allowed, score_scale):
    scores = low_back(jnp.einsum('bqhd,bkhd->bhqk', queries, keys_all, precision=HIGH) * score_scale)
    if allowed is not None:
        scores = jnp.where(allowed, scores, NEGATIVE)
    probability = low(jax.nn.softmax(scores, axis=-1))
    return low(low_back(jnp.einsum('bhqk,bkhd->bqhd', probability, values_all, precision=HIGH)))

def block(residual, params, head_count, allowed, score_scale):
    norm_gain, norm_bias, w_qkv, w_proj, mlp_gain, mlp_bias, w_up, w_down = params
    groups, length, model_width = residual.shape
    head_dim = model_width // head_count
    resid_flat = residual.reshape(groups * length, model_width)
    normed = low(norm_rows(resid_flat, norm_gain, norm_bias))
    packed = low(low_back(product(normed, w_qkv))).reshape(groups, length, 3, head_count, head_dim)
    context = attention_core(packed[:, :, 0], packed[:, :, 1], packed[:, :, 2], allowed, score_scale)
    middle = resid_flat + low_back(product(context.reshape(groups * length, model_width), w_proj))
    normed_two = low(norm_rows(middle, mlp_gain, mlp_bias))
    hidden_act = low(jax.nn.gelu(low_back(product(normed_two, w_up)), approximate=False))
    output = middle + low_back(product(hidden_act, w_down))
    return output.reshape(groups, length, model_width)

def segments(visible_counts):
    image_ends = jnp.cumsum(visible_counts, axis=1).astype(jnp.int32)
    position = jnp.arange(SEQ).astype(jnp.int32)
    return lax.optimization_barrier(jnp.sum((image_ends[:, None, :] <= position[None, :, None]).astype(jnp.int32), axis=2)).astype(jnp.int32)

def forward(inputs, enc_params, embed_weight, mask_token, dec_params, visible_counts, patch_positions, image_owner):
    segment_ids = segments(visible_counts)
    per_step = min(N_WIDE, max(1, 4096 // SEQ))
    enc_scale = HEAD_DIM ** (-0.5)

    def encode(group_pair):
        group_rows, group_ids = group_pair
        allowed = group_ids[:, None, :, None] == group_ids[:, None, None, :]
        return block(group_rows, enc_params, HEADS, allowed, enc_scale)
    encoded = lax.map(jax.checkpoint(encode), (inputs.reshape(N_WIDE // per_step, per_step, SEQ, D), segment_ids.reshape(N_WIDE // per_step, per_step, SEQ)))
    embedded = low(low_back(product(low(encoded.reshape(N_WIDE * SEQ, D)), embed_weight)))
    image_global = (jnp.arange(N_WIDE).astype(jnp.int32)[:, None] * IMG_SEQ + segment_ids).reshape(-1).astype(jnp.int32)
    target = (image_owner[image_global] * PATCHES + patch_positions.reshape(-1)).astype(jnp.int32)
    region = IMAGES * PATCHES
    placed = jnp.zeros((region, DD), jnp.float32).at[target].set(embedded)
    visible_slot = jnp.zeros((region,), jnp.float32).at[target].set(1.0)
    start_rows = jnp.where(visible_slot[:, None] > 0, placed, mask_token[None, :])
    dec_input = start_rows.reshape(IMAGES, PATCHES, DD) + position_table(DD)[None]
    dec_scale = DHEAD_DIM ** (-0.5)

    def decode(group_rows):
        return block(group_rows, dec_params, DHEADS, None, dec_scale)
    decoded = lax.map(jax.checkpoint(decode), dec_input.reshape(N_WIDE, IMG_SEQ, PATCHES, DD))
    return decoded.reshape(IMAGES, PATCHES, DD)

def reference(inputs, enc_norm_gain, enc_norm_bias, enc_qkv, enc_proj, enc_mlp_gain, enc_mlp_bias, enc_up, enc_down, embed_weight, mask_token, dec_norm_gain, dec_norm_bias, dec_qkv, dec_proj, dec_mlp_gain, dec_mlp_bias, dec_up, dec_down, cotangent, visible_counts, patch_positions, image_owner):
    floats = [value_arg.astype(jnp.float32) for value_arg in (inputs, enc_norm_gain, enc_norm_bias, enc_qkv, enc_proj, enc_mlp_gain, enc_mlp_bias, enc_up, enc_down, embed_weight, mask_token, dec_norm_gain, dec_norm_bias, dec_qkv, dec_proj, dec_mlp_gain, dec_mlp_bias, dec_up, dec_down)]

    def run_layer(*values):
        return forward(values[0], tuple(values[1:9]), values[9], values[10], tuple(values[11:19]), visible_counts, patch_positions, image_owner)
    decoded, pullback = jax.vjp(run_layer, *floats)
    gradients = pullback(cotangent.astype(jnp.float32))
    return (decoded.astype(jnp.bfloat16), gradients[0], gradients[1], gradients[2], gradients[3], gradients[4], gradients[5], gradients[6], gradients[7], gradients[8], gradients[9], gradients[10], gradients[11], gradients[12], gradients[13], gradients[14], gradients[15], gradients[16], gradients[17], gradients[18])
```

```python
import math

import jax
import jax.numpy as jnp
from jax import lax
from jax.sharding import PartitionSpec as P

HEADS = 12
HEAD_DIM = 64
DD = 512
DHEADS = 16
DHEAD_DIM = 32
PATCHES = 196
SEQ = 1024
IMG_SEQ = 16


EPSILON = 1e-06
NEGATIVE = -1e30


def product(left_side, right_side):
    return jnp.dot(left_side, right_side, preferred_element_type=jnp.float32)


def outer_sum(left_side, right_side):
    return lax.dot_general(
        left_side, right_side, (((0,), (0,)), ((), ())), preferred_element_type=jnp.float32
    )


def back_product(grad_rows, weight):
    return lax.dot_general(
        grad_rows, weight, (((1,), (1,)), ((), ())), preferred_element_type=jnp.float32
    )


def norm_rows(values, norm_gain, norm_bias):
    center = values - jnp.mean(values, axis=-1, keepdims=True)
    scaled = center * lax.rsqrt(jnp.mean(center * center, axis=-1, keepdims=True) + EPSILON)
    return scaled * norm_gain.astype(jnp.float32) + norm_bias.astype(jnp.float32)


def exact_gelu(values):
    return jax.nn.gelu(values, approximate=False)


def position_table(model_width):
    grid_side = math.isqrt(PATCHES)
    patch_index = jnp.arange(PATCHES)
    row_coord = (patch_index // grid_side).astype(jnp.float32)[:, None]
    col_coord = (patch_index % grid_side).astype(jnp.float32)[:, None]
    quarter = model_width // 4
    frequency = jnp.power(10000.0, -jnp.arange(quarter).astype(jnp.float32) / quarter)[None, :]
    return jnp.concatenate(
        [
            jnp.sin(row_coord * frequency),
            jnp.cos(row_coord * frequency),
            jnp.sin(col_coord * frequency),
            jnp.cos(col_coord * frequency),
        ],
        axis=1,
    )


def score_rows(queries, keys_all, allowed, score_scale):
    scores = (
        jnp.einsum("bqhd,bkhd->bhqk", queries, keys_all, preferred_element_type=jnp.float32)
        * score_scale
    )
    if allowed is None:
        return scores
    return jnp.where(allowed, scores, NEGATIVE)


def attend(queries, keys_all, values_all, allowed, score_scale):
    scores = score_rows(queries, keys_all, allowed, score_scale)
    highest = jnp.max(scores, axis=-1, keepdims=True)
    raised = jnp.exp(scores - highest)
    totals = jnp.sum(raised, axis=-1, keepdims=True)
    weights = (raised / totals).astype(jnp.bfloat16)
    context = jnp.einsum("bhqk,bkhd->bqhd", weights, values_all, preferred_element_type=jnp.float32)
    return (context.astype(jnp.bfloat16), highest, totals)


def attend_back(queries, keys_all, values_all, allowed, score_scale, highest, totals, d_context):
    scores = score_rows(queries, keys_all, allowed, score_scale)
    probability = jnp.exp(scores - highest) / totals
    d_probs = jnp.einsum(
        "bqhd,bkhd->bhqk", d_context, values_all, preferred_element_type=jnp.float32
    )
    row_inner = jnp.sum(probability * d_probs, axis=-1, keepdims=True)
    d_scores = (probability * (d_probs - row_inner)).astype(jnp.bfloat16)
    d_queries = (
        jnp.einsum("bhqk,bkhd->bqhd", d_scores, keys_all, preferred_element_type=jnp.float32)
        * score_scale
    )
    d_keys = (
        jnp.einsum("bhqk,bqhd->bkhd", d_scores, queries, preferred_element_type=jnp.float32)
        * score_scale
    )
    d_values = jnp.einsum(
        "bhqk,bqhd->bkhd",
        probability.astype(jnp.bfloat16),
        d_context,
        preferred_element_type=jnp.float32,
    )
    return (d_queries, d_keys, d_values)


def block_forward(residual, params, head_count, share_keys, allowed, score_scale):
    norm_gain, norm_bias, w_qkv, w_proj, mlp_gain, mlp_bias, w_up, w_down = params
    groups, length, model_width = residual.shape
    head_dim = model_width // head_count
    resid_flat = residual.reshape(groups * length, model_width)
    normed = norm_rows(resid_flat, norm_gain, norm_bias).astype(jnp.bfloat16)
    packed = (
        product(normed, w_qkv).astype(jnp.bfloat16).reshape(groups, length, 3, head_count, head_dim)
    )
    queries = packed[:, :, 0]
    keys_all, values_all = share_keys(packed[:, :, 1], packed[:, :, 2])
    context, highest, totals = attend(queries, keys_all, values_all, allowed, score_scale)
    context_flat = context.reshape(groups * length, model_width)
    middle = resid_flat + product(context_flat, w_proj)
    normed_two = norm_rows(middle, mlp_gain, mlp_bias).astype(jnp.bfloat16)
    hidden_pre = product(normed_two, w_up)
    hidden_act = exact_gelu(hidden_pre).astype(jnp.bfloat16)
    output = middle + product(hidden_act, w_down)
    saved_state = (
        resid_flat,
        normed,
        queries,
        keys_all,
        values_all,
        highest,
        totals,
        context_flat,
        middle,
        normed_two,
        hidden_pre,
        hidden_act,
    )
    return (output, saved_state)


def block_backward(d_output, saved_state, params, unshare_keys, allowed, score_scale):
    norm_gain, norm_bias, w_qkv, w_proj, mlp_gain, mlp_bias, w_up, w_down = params
    (
        resid_flat,
        normed,
        queries,
        keys_all,
        values_all,
        highest,
        totals,
        context_flat,
        middle,
        normed_two,
        hidden_pre,
        hidden_act,
    ) = saved_state
    groups, length = (queries.shape[0], queries.shape[1])
    d_branch = d_output.astype(jnp.bfloat16)
    grad_down = outer_sum(hidden_act, d_branch)
    d_act = back_product(d_branch, w_down)
    gelu_back = jax.vjp(exact_gelu, hidden_pre)[1]
    d_pre = gelu_back(d_act)[0].astype(jnp.bfloat16)
    grad_up = outer_sum(normed_two, d_pre)
    d_normed_two = back_product(d_pre, w_up)
    mlp_back = jax.vjp(
        norm_rows, middle, mlp_gain.astype(jnp.float32), mlp_bias.astype(jnp.float32)
    )[1]
    d_mid_part, grad_mlp_gain, grad_mlp_bias = mlp_back(d_normed_two)
    d_middle = d_output + d_mid_part
    d_attn = d_middle.astype(jnp.bfloat16)
    grad_proj = outer_sum(context_flat, d_attn)
    d_context = back_product(d_attn, w_proj).astype(jnp.bfloat16).reshape(queries.shape)
    d_queries, d_keys_all, d_values_all = attend_back(
        queries, keys_all, values_all, allowed, score_scale, highest, totals, d_context
    )
    d_keys, d_values = unshare_keys(d_keys_all, d_values_all)
    d_packed = (
        jnp.stack([d_queries, d_keys, d_values], axis=2)
        .astype(jnp.bfloat16)
        .reshape(groups * length, -1)
    )
    grad_qkv = outer_sum(normed, d_packed)
    d_normed = back_product(d_packed, w_qkv)
    norm_back = jax.vjp(
        norm_rows, resid_flat, norm_gain.astype(jnp.float32), norm_bias.astype(jnp.float32)
    )[1]
    d_resid_part, grad_norm_gain, grad_norm_bias = norm_back(d_normed)
    return (
        d_middle + d_resid_part,
        (
            grad_norm_gain,
            grad_norm_bias,
            grad_qkv,
            grad_proj,
            grad_mlp_gain,
            grad_mlp_bias,
            grad_up,
            grad_down,
        ),
    )


def keep_local(first_part, second_part):
    return (first_part, second_part)


SWAP = [(0, 1), (1, 0)]
GATHER_ORDERS = ((0, 2, 1), (0, 1, 2), (2, 1, 0))


class Grid:
    def __init__(self, wide):
        dims, at = [1, 1, 1], 0
        while wide > 1:
            dims[at % 3] *= 2
            wide //= 2
            at += 1
        self.dims = tuple(dims)
        self.wide = dims[0] * dims[1] * dims[2]

    def split(self, wide_index):
        _, rows, cols = self.dims
        return (wide_index // (rows * cols), (wide_index // cols) % rows, wide_index % cols)

    def ring(self, axis):
        size = self.dims[axis]
        order = list(range(0, size, 2)) + list(range(size - 1, 0, -2))
        following = {order[k]: order[(k + 1) % size] for k in range(size)}
        pairs = []
        for source in range(self.wide):
            place = list(self.split(source))
            place[axis] = following[place[axis]]
            pairs.append((source, (place[0] * self.dims[1] + place[1]) * self.dims[2] + place[2]))
        return pairs

    def own(self, axis):
        return self.split(lax.axis_index("wide"))[axis]

    def behind(self, axis, steps):
        size, own = self.dims[axis], self.own(axis)
        if size == 2:
            return (own + steps) % 2
        place = jnp.where(own % 2 == 0, own // 2, size - 1 - own // 2)
        place = (place - steps + size) % size
        return jnp.where(place < size // 2, 2 * place, 2 * (size - place) - 1)


def gather_axis(grid, block, axis):
    size = grid.dims[axis]
    if size == 1:
        return block
    shape = list(block.shape)
    shape[axis] = size
    whole = jnp.zeros(tuple(shape), block.dtype)
    whole = lax.dynamic_update_slice_in_dim(whole, block, grid.own(axis), axis)
    for step in range(1, size):
        block = lax.ppermute(block, "wide", grid.ring(axis))
        whole = lax.dynamic_update_slice_in_dim(whole, block, grid.behind(axis, step), axis)
    return whole


def scatter_axis(grid, terms, axis):
    size = grid.dims[axis]
    if size == 1:
        return terms.astype(jnp.float32)

    def term(step):
        part = lax.dynamic_slice_in_dim(terms, grid.behind(axis, step % size), 1, axis)
        return part.astype(jnp.float32)

    total = term(1)
    for step in range(2, size + 1):
        got = lax.ppermute(total.astype(jnp.bfloat16), "wide", grid.ring(axis))
        total = got.astype(jnp.float32) + term(step)
    return total


def gather_parts(grid, parts):
    gathered = []
    for k, part in enumerate(parts):
        block = part[None, None, None]
        for axis in GATHER_ORDERS[k % 3]:
            block = gather_axis(grid, block, axis)
        gathered.append(block.reshape((grid.wide,) + part.shape))
    return gathered


def scatter_parts(grid, parts):
    scattered = []
    for k, part in enumerate(parts):
        block = part.reshape(grid.dims + part.shape[1:])
        for axis in GATHER_ORDERS[k % 3][::-1]:
            block = scatter_axis(grid, block, axis)
        scattered.append(block.reshape(part.shape[1:]))
    return scattered


def halves(array, core):
    width = array.shape[-1] // 2
    own = lax.dynamic_slice_in_dim(array, core * width, width, array.ndim - 1)
    other = lax.dynamic_slice_in_dim(array, (1 - core) * width, width, array.ndim - 1)
    return own, other


def in_order(own, other, core, axis):
    return jnp.where(
        core == 0,
        jnp.concatenate([own, other], axis=axis),
        jnp.concatenate([other, own], axis=axis),
    )


def chip_rows(array, core):
    own, other = halves(array, core)
    return in_order(own, lax.ppermute(other, "narrow", SWAP), core, 0)


def core_rows(array, core):
    rows = array.shape[0] // 2
    own = lax.dynamic_slice_in_dim(array, core * rows, rows, 0)
    other = lax.dynamic_slice_in_dim(array, (1 - core) * rows, rows, 0)
    return in_order(own, lax.ppermute(other, "narrow", SWAP), core, 1)


def shards(
    inputs,
    enc_norm_gain,
    enc_norm_bias,
    enc_qkv,
    enc_proj,
    enc_mlp_gain,
    enc_mlp_bias,
    enc_up,
    enc_down,
    embed_weight,
    mask_token,
    dec_norm_gain,
    dec_norm_bias,
    dec_qkv,
    dec_proj,
    dec_mlp_gain,
    dec_mlp_bias,
    dec_up,
    dec_down,
    cotangent,
    visible_counts,
    patch_positions,
    image_owner,
):
    narrow_index = lax.axis_index("narrow")
    wide_index = lax.axis_index("wide")
    half_rows = inputs.shape[1]
    narrow_count = lax.axis_size("narrow")
    slot_count = IMG_SEQ // narrow_count
    region = slot_count * PATCHES
    image_ends = jnp.cumsum(visible_counts[0], axis=0)
    position = jnp.arange(SEQ, dtype=jnp.int32)
    segment_all = jnp.sum((image_ends[None, :] <= position[:, None]).astype(jnp.int32), axis=1)
    segment_own = lax.dynamic_slice_in_dim(segment_all, narrow_index * half_rows, half_rows, 0)

    def share_sequence(keys_own, values_own):
        return (
            lax.all_gather(keys_own, "narrow", axis=1, tiled=True),
            lax.all_gather(values_own, "narrow", axis=1, tiled=True),
        )

    def unshare_sequence(d_keys_all, d_values_all):
        return (
            lax.psum_scatter(
                d_keys_all.astype(jnp.bfloat16), "narrow", scatter_dimension=1, tiled=True
            ).astype(jnp.float32),
            lax.psum_scatter(
                d_values_all.astype(jnp.bfloat16), "narrow", scatter_dimension=1, tiled=True
            ).astype(jnp.float32),
        )

    allowed = (segment_own[:, None] == segment_all[None, :])[None, None]

    grid = Grid(lax.axis_size("wide"))
    device_count = grid.wide * narrow_count
    rows_e, rows_d = enc_qkv.shape[0], dec_qkv.shape[0]
    width_e, width_d = enc_proj.shape[1], dec_proj.shape[1]
    wide_e, wide_d = enc_up.shape[1], dec_up.shape[1]

    vectors_e = jnp.stack([enc_norm_gain, enc_norm_bias, enc_mlp_gain, enc_mlp_bias], axis=1)
    vectors_d = jnp.stack(
        [dec_norm_gain, dec_norm_bias, dec_mlp_gain, dec_mlp_bias, mask_token], axis=1
    )
    vectors = jnp.concatenate(
        [
            jnp.pad(vectors_e, ((0, 0), (0, 124))),
            jnp.pad(vectors_d, ((0, rows_e - rows_d), (0, 123))),
        ],
        axis=1,
    )
    down_groups = dec_down.shape[0] // rows_d
    dec_packed = jnp.concatenate(
        [
            dec_qkv,
            dec_proj,
            dec_up,
            dec_down.reshape(down_groups, rows_d, width_d)
            .transpose(1, 0, 2)
            .reshape(rows_d, down_groups * width_d),
        ],
        axis=1,
    )
    dec_whole = lax.all_gather(dec_packed, ("wide", "narrow"), axis=0, tiled=True)

    enc_halves = [chip_rows(w, narrow_index) for w in (enc_qkv, enc_proj, enc_up, embed_weight, vectors)]
    cut = enc_halves[2].shape[1] // 2
    column_parts = [
        enc_halves[0],
        jnp.concatenate([enc_halves[1], enc_halves[2][:, :cut]], axis=1),
        jnp.concatenate([enc_halves[2][:, cut:], enc_halves[3], enc_halves[4]], axis=1),
    ]
    down_half = chip_rows(enc_down, narrow_index)
    third = down_half.shape[0] // 3
    row_parts = [down_half[k * third : (k + 1) * third] for k in range(3)]
    wide_parts = gather_parts(grid, column_parts + row_parts)
    other_parts = [lax.ppermute(part, "narrow", SWAP) for part in wide_parts]
    low_parts = [jnp.where(narrow_index == 0, a, b) for a, b in zip(wide_parts, other_parts)]
    high_parts = [jnp.where(narrow_index == 0, b, a) for a, b in zip(wide_parts, other_parts)]

    def both(part, start, stop):
        return jnp.concatenate(
            [low_parts[part][:, :, start:stop], high_parts[part][:, :, start:stop]], axis=2
        ).reshape(device_count * rows_e, 2 * (stop - start))

    half_p, half_v = width_e // 2, enc_halves[3].shape[1]
    full_qkv = jnp.concatenate([low_parts[0], high_parts[0]], axis=2).reshape(width_e, 3 * width_e)
    full_proj = both(1, 0, half_p)
    full_up = jnp.concatenate(
        [
            low_parts[1][:, :, half_p:],
            low_parts[2][:, :, :cut],
            high_parts[1][:, :, half_p:],
            high_parts[2][:, :, :cut],
        ],
        axis=2,
    ).reshape(width_e, wide_e)
    w_embed = both(2, cut, cut + half_v)
    enc_vec = low_parts[2][:, :, cut + half_v :].reshape(width_e, 128)
    dec_vec = (
        high_parts[2][:, :, cut + half_v :]
        .reshape(device_count, rows_e, 128)[:, :rows_d]
        .reshape(width_d, 128)
    )
    full_down = jnp.concatenate(
        [jnp.concatenate([a, b], axis=2) for a, b in zip(low_parts[3:], high_parts[3:])], axis=1
    ).reshape(wide_e, width_e)
    enc_params = (
        enc_vec[:, 0],
        enc_vec[:, 1],
        full_qkv,
        full_proj,
        enc_vec[:, 2],
        enc_vec[:, 3],
        full_up,
        full_down,
    )
    at_d = [0, 3 * width_d, 4 * width_d, 4 * width_d + wide_d]
    dec_params = (
        dec_vec[:, 0],
        dec_vec[:, 1],
        dec_whole[:, at_d[0] : at_d[1]],
        dec_whole[:, at_d[1] : at_d[2]],
        dec_vec[:, 2],
        dec_vec[:, 3],
        dec_whole[:, at_d[2] : at_d[3]],
        dec_whole[:, at_d[3] :]
        .reshape(device_count, rows_d, down_groups, width_d)
        .transpose(0, 2, 1, 3)
        .reshape(wide_d, width_d),
    )
    mask_vector = dec_vec[:, 4].astype(jnp.float32)

    enc_scale = HEAD_DIM ** (-0.5)
    dec_scale = DHEAD_DIM ** (-0.5)
    residual = inputs.astype(jnp.float32)
    encoded, enc_saved = block_forward(
        residual, enc_params, HEADS, share_sequence, allowed, enc_scale
    )
    encoded_low = encoded.astype(jnp.bfloat16)
    embedded = product(encoded_low, w_embed).astype(jnp.bfloat16)
    image_global = wide_index * IMG_SEQ + segment_own
    owner_value = image_owner[image_global]
    destination = owner_value // slot_count - wide_index * narrow_count
    slot_index = owner_value % slot_count
    send_index = destination * half_rows + jnp.arange(half_rows, dtype=jnp.int32)
    send_rows = jnp.zeros((narrow_count * half_rows, DD), jnp.bfloat16).at[send_index].set(embedded)
    send_meta = (
        jnp.full((narrow_count * half_rows,), -1, jnp.int32)
        .at[send_index]
        .set(slot_index * PATCHES + patch_positions[0])
    )
    got_rows, got_meta = (
        lax.all_to_all(
            send_rows.reshape(narrow_count, half_rows, DD),
            "narrow",
            split_axis=0,
            concat_axis=0,
            tiled=True,
        ),
        lax.all_to_all(
            send_meta.reshape(narrow_count, half_rows),
            "narrow",
            split_axis=0,
            concat_axis=0,
            tiled=True,
        ),
    )
    meta_flat = got_meta.reshape(-1)
    target = jnp.where(meta_flat >= 0, meta_flat, region)
    placed = (
        jnp.zeros((region + 1, DD), jnp.float32)
        .at[target]
        .set(got_rows.reshape(-1, DD).astype(jnp.float32))
    )
    visible_slot = jnp.zeros((region + 1,), jnp.float32).at[target].set(1.0)[:region]
    start_rows = jnp.where(visible_slot[:, None] > 0, placed[:region], mask_vector[None, :])
    dec_input = start_rows.reshape(slot_count, PATCHES, DD) + position_table(DD)[None]
    dec_out, dec_saved = block_forward(dec_input, dec_params, DHEADS, keep_local, None, dec_scale)
    decoded = dec_out.reshape(slot_count, PATCHES, DD).astype(jnp.bfloat16)
    d_dec_out = cotangent.astype(jnp.float32).reshape(region, DD)
    d_start, dec_grads = block_backward(
        d_dec_out, dec_saved, dec_params, keep_local, None, dec_scale
    )
    grad_mask = jnp.sum(jnp.where(visible_slot[:, None] > 0, 0.0, d_start), axis=0)
    padded_grad = jnp.concatenate([d_start, jnp.zeros((1, DD), jnp.float32)], axis=0)
    d_sent = padded_grad[target].astype(jnp.bfloat16).reshape(narrow_count, half_rows, DD)
    d_back = lax.all_to_all(d_sent, "narrow", split_axis=0, concat_axis=0, tiled=True)
    d_embedded = d_back.reshape(narrow_count * half_rows, DD)[send_index]
    grad_embed = outer_sum(encoded_low, d_embedded)
    d_encoded = back_product(d_embedded, w_embed)
    d_inputs, enc_grads = block_backward(
        d_encoded, enc_saved, enc_params, unshare_sequence, allowed, enc_scale
    )
    low = jnp.bfloat16

    def chip_blocks(array):
        own, other = halves(array, narrow_index)
        got = lax.ppermute(other.astype(low), "narrow", SWAP)
        total = own.astype(jnp.float32) + got.astype(jnp.float32)
        return total.reshape(grid.wide, -1, total.shape[-1])

    grad_vec_e = jnp.stack([enc_grads[0], enc_grads[1], enc_grads[4], enc_grads[5]], axis=1)
    grad_vec_d = jnp.stack(
        [dec_grads[0], dec_grads[1], dec_grads[4], dec_grads[5], grad_mask], axis=1
    ).reshape(device_count, rows_d, 5)
    grad_vec = jnp.concatenate(
        [
            jnp.pad(grad_vec_e, ((0, 0), (0, 124))),
            jnp.pad(grad_vec_d, ((0, 0), (0, rows_e - rows_d), (0, 123))).reshape(width_e, 128),
        ],
        axis=1,
    )
    dec_grad_packed = jnp.concatenate(
        [
            dec_grads[2].astype(low),
            dec_grads[3].astype(low),
            dec_grads[6].astype(low),
            dec_grads[7]
            .astype(low)
            .reshape(device_count, down_groups, rows_d, width_d)
            .transpose(0, 2, 1, 3)
            .reshape(width_d, down_groups * width_d),
        ],
        axis=1,
    )
    dec_sum = lax.psum_scatter(
        dec_grad_packed, ("wide", "narrow"), scatter_dimension=0, tiled=True
    ).astype(jnp.float32)
    chip_qkv, chip_proj, chip_up, chip_embed, chip_vec, chip_down = [
        chip_blocks(g)
        for g in (enc_grads[2], enc_grads[3], enc_grads[6], grad_embed, grad_vec, enc_grads[7])
    ]
    sums = scatter_parts(
        grid,
        [
            chip_qkv,
            jnp.concatenate([chip_proj, chip_up[:, :, :cut]], axis=2),
            jnp.concatenate([chip_up[:, :, cut:], chip_embed, chip_vec], axis=2),
        ]
        + [chip_down[:, k * third : (k + 1) * third] for k in range(3)],
    )
    out_qkv = core_rows(sums[0], narrow_index)
    out_proj = core_rows(sums[1][:, :half_p], narrow_index)
    out_up = core_rows(jnp.concatenate([sums[1][:, half_p:], sums[2][:, :cut]], axis=1), narrow_index)
    out_embed = core_rows(sums[2][:, cut : cut + half_v], narrow_index)
    out_vec = core_rows(sums[2][:, cut + half_v :], narrow_index)
    out_down = core_rows(jnp.concatenate(sums[3:], axis=0), narrow_index)
    out_vec_d = out_vec[:rows_d, 128:133]
    return (
        decoded,
        d_inputs.reshape(inputs.shape),
        out_vec[:, 0],
        out_vec[:, 1],
        out_qkv,
        out_proj,
        out_vec[:, 2],
        out_vec[:, 3],
        out_up,
        out_down,
        out_embed,
        out_vec_d[:, 4],
        out_vec_d[:, 0],
        out_vec_d[:, 1],
        dec_sum[:, at_d[0] : at_d[1]],
        dec_sum[:, at_d[1] : at_d[2]],
        out_vec_d[:, 2],
        out_vec_d[:, 3],
        dec_sum[:, at_d[2] : at_d[3]],
        dec_sum[:, at_d[3] :]
        .reshape(rows_d, down_groups, width_d)
        .transpose(1, 0, 2)
        .reshape(rows_d * down_groups, width_d),
    )


def solution(mesh):
    in_specs = (
        P("wide", "narrow", None),
        P(("wide", "narrow")),
        P(("wide", "narrow")),
        P(("wide", "narrow"), None),
        P(("wide", "narrow"), None),
        P(("wide", "narrow")),
        P(("wide", "narrow")),
        P(("wide", "narrow"), None),
        P(("wide", "narrow"), None),
        P(("wide", "narrow"), None),
        P(("wide", "narrow")),
        P(("wide", "narrow")),
        P(("wide", "narrow")),
        P(("wide", "narrow"), None),
        P(("wide", "narrow"), None),
        P(("wide", "narrow")),
        P(("wide", "narrow")),
        P(("wide", "narrow"), None),
        P(("wide", "narrow"), None),
        P(("wide", "narrow"), None, None),
        P("wide", None),
        P("wide", "narrow"),
        P(),
    )
    out_specs = (
        P(("wide", "narrow"), None, None),
        P("wide", "narrow", None),
        P(("wide", "narrow")),
        P(("wide", "narrow")),
        P(("wide", "narrow"), None),
        P(("wide", "narrow"), None),
        P(("wide", "narrow")),
        P(("wide", "narrow")),
        P(("wide", "narrow"), None),
        P(("wide", "narrow"), None),
        P(("wide", "narrow"), None),
        P(("wide", "narrow")),
        P(("wide", "narrow")),
        P(("wide", "narrow")),
        P(("wide", "narrow"), None),
        P(("wide", "narrow"), None),
        P(("wide", "narrow")),
        P(("wide", "narrow")),
        P(("wide", "narrow"), None),
        P(("wide", "narrow"), None),
    )
    return jax.shard_map(shards, mesh=mesh, in_specs=in_specs, out_specs=out_specs, check_vma=False)
```

```python
import math

import jax
import jax.numpy as jnp
from jax import lax
from jax.experimental import pallas as pl
from jax.experimental.pallas import tpu as pltpu
from jax.sharding import PartitionSpec as P

HEADS = 12
HEAD_DIM = 64
DD = 512
DHEADS = 16
DHEAD_DIM = 32
PATCHES = 196
SEQ = 1024
IMG_SEQ = 16


EPSILON = 1e-06
NEGATIVE = -1e30


def position_table(model_width):
    grid_side = math.isqrt(PATCHES)
    patch_index = jnp.arange(PATCHES)
    row_coord = (patch_index // grid_side).astype(jnp.float32)[:, None]
    col_coord = (patch_index % grid_side).astype(jnp.float32)[:, None]
    quarter = model_width // 4
    frequency = jnp.power(10000.0, -jnp.arange(quarter).astype(jnp.float32) / quarter)[None, :]
    return jnp.concatenate(
        [
            jnp.sin(row_coord * frequency),
            jnp.cos(row_coord * frequency),
            jnp.sin(col_coord * frequency),
            jnp.cos(col_coord * frequency),
        ],
        axis=1,
    )


SWAP = [(0, 1), (1, 0)]
GATHER_ORDERS = ((0, 2, 1), (0, 1, 2), (2, 1, 0))


class Grid:
    def __init__(self, wide):
        dims, at = [1, 1, 1], 0
        while wide > 1:
            dims[at % 3] *= 2
            wide //= 2
            at += 1
        self.dims = tuple(dims)
        self.wide = dims[0] * dims[1] * dims[2]

    def split(self, wide_index):
        _, rows, cols = self.dims
        return (wide_index // (rows * cols), (wide_index // cols) % rows, wide_index % cols)

    def ring(self, axis):
        size = self.dims[axis]
        order = list(range(0, size, 2)) + list(range(size - 1, 0, -2))
        following = {order[k]: order[(k + 1) % size] for k in range(size)}
        pairs = []
        for source in range(self.wide):
            place = list(self.split(source))
            place[axis] = following[place[axis]]
            pairs.append((source, (place[0] * self.dims[1] + place[1]) * self.dims[2] + place[2]))
        return pairs

    def own(self, axis):
        return self.split(lax.axis_index("wide"))[axis]

    def behind(self, axis, steps):
        size, own = self.dims[axis], self.own(axis)
        if size == 2:
            return (own + steps) % 2
        place = jnp.where(own % 2 == 0, own // 2, size - 1 - own // 2)
        place = (place - steps + size) % size
        return jnp.where(place < size // 2, 2 * place, 2 * (size - place) - 1)


def gather_axis(grid, block, axis):
    size = grid.dims[axis]
    if size == 1:
        return block
    shape = list(block.shape)
    shape[axis] = size
    whole = jnp.zeros(tuple(shape), block.dtype)
    whole = lax.dynamic_update_slice_in_dim(whole, block, grid.own(axis), axis)
    for step in range(1, size):
        block = lax.ppermute(block, "wide", grid.ring(axis))
        whole = lax.dynamic_update_slice_in_dim(whole, block, grid.behind(axis, step), axis)
    return whole


def scatter_axis(grid, terms, axis):
    size = grid.dims[axis]

    def term(step):
        at = grid.behind(axis, step % size)
        slices = [lax.dynamic_slice_in_dim(t, at, 1, axis).astype(jnp.float32) for t in terms]
        return sum(slices[1:], slices[0])

    if size == 1:
        return sum([t.astype(jnp.float32) for t in terms[1:]], terms[0].astype(jnp.float32))
    total = term(1)
    for step in range(2, size + 1):
        got = lax.ppermute(total.astype(jnp.bfloat16), "wide", grid.ring(axis))
        total = got.astype(jnp.float32) + term(step)
    return total


def gather_parts(grid, parts):
    gathered = []
    for k, part in enumerate(parts):
        block = part[None, None, None]
        for axis in GATHER_ORDERS[k % 3]:
            block = gather_axis(grid, block, axis)
        gathered.append(block.reshape((grid.wide,) + part.shape))
    return gathered


def scatter_part(grid, terms, order):
    columns = terms[0].shape[-1]
    terms = [t.reshape(grid.dims + (-1, columns)) for t in terms]
    for axis in order:
        terms = [scatter_axis(grid, terms, axis)]
    return terms[0].reshape(-1, columns)


def regroup(array, block, start, width, groups=None):
    blocks, old = array.shape[:2]
    if old == block:
        return array
    groups = groups or (array.shape[2] - start) // width
    stop = start + groups * width
    rows = array[:, :, start:stop].reshape(blocks, old, groups, width).transpose(0, 2, 1, 3)
    rows = rows.reshape(-1, groups, block, width).transpose(0, 2, 1, 3).reshape(-1, block, groups * width)
    sides = [array[:, :, :start], array[:, :, stop:]]
    sides = [x.reshape(-1, block, x.shape[2]) if x.shape[2] else None for x in sides]
    return jnp.concatenate([x for x in (sides[0], rows, sides[1]) if x is not None], axis=2)


def halves(array, core):
    width = array.shape[-1] // 2
    own = lax.dynamic_slice_in_dim(array, core * width, width, array.ndim - 1)
    other = lax.dynamic_slice_in_dim(array, (1 - core) * width, width, array.ndim - 1)
    return own, other


def in_order(own, other, core, axis):
    return jnp.where(
        core == 0,
        jnp.concatenate([own, other], axis=axis),
        jnp.concatenate([other, own], axis=axis),
    )


def chip_rows(array, core):
    own, other = halves(array, core)
    return in_order(own, lax.ppermute(other, "narrow", SWAP), core, 0)


def core_rows(array, core):
    rows = array.shape[0] // 2
    own = lax.dynamic_slice_in_dim(array, core * rows, rows, 0)
    other = lax.dynamic_slice_in_dim(array, (1 - core) * rows, rows, 0)
    return in_order(own, lax.ppermute(other, "narrow", SWAP), core, 1)


ENC_BLOCK = 48
DEC_BLOCK = 16
LOG2E = 1.4426950408889634
PAD = 208
LIMIT = 56 * 2**20


def dot_nn(a, b):
    return jnp.dot(a, b, preferred_element_type=jnp.float32)


def dot_nt(a, b):
    return lax.dot_general(a, b, (((1,), (1,)), ((), ())), preferred_element_type=jnp.float32)


def dot_tn(a, b):
    return lax.dot_general(a, b, (((0,), (0,)), ((), ())), preferred_element_type=jnp.float32)


def low(values):
    return values.astype(jnp.bfloat16)


def norm_stats(values):
    center = values - jnp.mean(values, axis=-1, keepdims=True)
    scale = lax.rsqrt(jnp.mean(center * center, axis=-1, keepdims=True) + EPSILON)
    return center * scale, scale


def norm_apply(values, gain, bias):
    unit, _ = norm_stats(values)
    return unit * gain + bias


def norm_back(values, gain, d_normed):
    unit, scale = norm_stats(values)
    d_unit = d_normed * gain
    mean_d = jnp.mean(d_unit, axis=-1, keepdims=True)
    mean_du = jnp.mean(d_unit * unit, axis=-1, keepdims=True)
    d_values = scale * (d_unit - mean_d - unit * mean_du)
    return (
        d_values,
        jnp.sum(d_normed * unit, axis=0, keepdims=True),
        jnp.sum(d_normed, axis=0, keepdims=True),
    )


def gelu_parts(u):
    size = jnp.abs(u)
    t = 1.0 / (1.0 + (0.3275911 * 0.7071067811865476) * size)
    bell = jnp.exp2(u * u * (-0.5 * LOG2E))
    tail = t * (
        0.127414796 + t * (-0.142248368 + t * (0.7107068705 + t * (-0.7265760135 + t * 0.5307027145)))
    )
    tail = tail * bell
    phi = jnp.where(u >= 0, 1.0 - tail, tail)
    return phi, u * bell * 0.3989422804014327


def full_spec(shape):
    zeros = (0,) * len(shape)
    return pl.BlockSpec(shape, lambda *_: zeros)


def lead_spec(shape, count):
    zeros = (0,) * (len(shape) - 1)
    return pl.BlockSpec((count,) + tuple(shape[1:]), lambda i: (i,) + zeros)


def call(body, grid, ins, in_specs, outs, out_specs, scratch, flops, name, aliases=None):
    moved = sum(x.size * x.dtype.itemsize for x in list(ins) + list(outs))
    return pl.pallas_call(
        body,
        grid=grid,
        in_specs=in_specs,
        out_specs=out_specs,
        out_shape=outs,
        scratch_shapes=scratch,
        compiler_params=pltpu.CompilerParams(vmem_limit_bytes=LIMIT),
        cost_estimate=pl.CostEstimate(flops=flops, bytes_accessed=moved, transcendentals=0),
        input_output_aliases=aliases or {},
        name=name,
    )(*ins)


def begin(pairs, sems, first=0):
    copies = [
        pltpu.make_async_copy(source, target, sems.at[first + k])
        for k, (source, target) in enumerate(pairs)
    ]
    for copy in copies:
        copy.start()
    return copies


def finish(copies):
    for copy in copies:
        copy.wait()


def lanes_of(core, width):
    return pl.ds(pl.multiple_of(core * width, 128), width)


ANY = pl.BlockSpec(memory_space=pl.ANY)
SMEM = pl.BlockSpec(memory_space=pltpu.SMEM)


def f32(*shape):
    return jax.ShapeDtypeStruct(shape, jnp.float32)


def b16(*shape):
    return jax.ShapeDtypeStruct(shape, jnp.bfloat16)


def place_head(rows, slot, count):
    pieces = []
    if slot:
        pieces.append(jnp.zeros((slot * rows.shape[0], rows.shape[1]), rows.dtype))
    pieces.append(rows)
    if slot < count - 1:
        pieces.append(jnp.zeros(((count - 1 - slot) * rows.shape[0], rows.shape[1]), rows.dtype))
    return jnp.concatenate(pieces, axis=0)


def keep_lanes(values, slot, width):
    lane = lax.broadcasted_iota(jnp.int32, values.shape, 1)
    inside = (lane >= slot * width) & (lane < (slot + 1) * width)
    return jnp.where(inside, values, jnp.zeros_like(values))


def dec_attention_body(
    key_ref, e_ref, posn_ref, vec_ref, wqkv_ref, wo_ref,
    z_ref, qkv_ref, o_ref, m_ref, p_ref, il_ref, ot_ref,
    qt_s, vt_s, ot_s,
):
    step = pl.program_id(0)
    count, rows, width = z_ref.shape
    heads = p_ref.shape[1]
    head = width // heads
    group = 128 // head
    kappa = head ** (-0.5) * LOG2E
    for j in range(count):
        wanted = lax.broadcasted_iota(jnp.int32, (rows, 1), 0) + (step * count + j) * 256
        match = (key_ref[...] == wanted).astype(jnp.float32)
        seen = jnp.sum(match, axis=1, keepdims=True)
        z_ref[j] = dot_nn(low(match), e_ref[...]) + (1.0 - seen) * vec_ref[4:5] + posn_ref[...]
    z = z_ref[...].reshape(count * rows, width)
    n1 = low(norm_apply(z, vec_ref[0:1], vec_ref[1:2]))
    qkv_ref[...] = low(dot_nn(n1, wqkv_ref[...])).reshape(count, rows, 3 * width)

    def one_image(j, carry):
        qt_s[...] = qkv_ref[j, :, 0:width].T
        vt_s[...] = qkv_ref[j, :, 2 * width : 3 * width].T
        for h in range(heads):
            quad, slot = divmod(h, group)
            keys = qkv_ref[j, :, width + 128 * quad : width + 128 * (quad + 1)]
            s = dot_nn(keys, place_head(qt_s[h * head : (h + 1) * head], slot, group))
            tail = lax.broadcasted_iota(jnp.int32, (16, rows), 0) < PATCHES - (rows - 16)
            s = jnp.concatenate([s[: rows - 16], jnp.where(tail, s[rows - 16 :], NEGATIVE)], axis=0)
            p = jnp.exp2((s - jnp.max(s, axis=0, keepdims=True)) * kappa)
            inverse = 1.0 / jnp.sum(p, axis=0, keepdims=True)
            p = low(p)
            p_ref[j, h] = p
            il_ref[j, h : h + 1] = inverse
            ot_s[h * head : (h + 1) * head] = dot_nn(vt_s[h * head : (h + 1) * head], p) * inverse
        ot_ref[j] = low(ot_s[...])
        o_ref[j] = low(ot_s[...].T)
        return carry

    lax.fori_loop(0, count, one_image, 0)
    m_ref[...] = (z + dot_nn(o_ref[...].reshape(count * rows, width), wo_ref[...])).reshape(
        count, rows, width
    )


def dec_attention(key, embedded, posn, vec, packed, images):
    width = packed.shape[0]
    two = 2
    outs = [
        f32(images, PAD, width),
        b16(images, PAD, 3 * width),
        b16(images, PAD, width),
        f32(images, PAD, width),
        b16(images, DHEADS, PAD, PAD),
        f32(images, DHEADS, PAD),
        b16(images, width, PAD),
    ]
    ins = [key, embedded, posn, vec, packed, packed]
    return call(
        dec_attention_body,
        (images // two,),
        ins,
        [full_spec(x.shape) for x in ins[:4]]
        + [pl.BlockSpec((width, 3 * width), lambda i: (0, 0)), pl.BlockSpec((width, width), lambda i: (0, 3))],
        outs,
        [lead_spec(x.shape, two) for x in outs],
        [
            pltpu.VMEM((width, PAD), jnp.bfloat16),
            pltpu.VMEM((width, PAD), jnp.bfloat16),
            pltpu.VMEM((width, PAD), jnp.float32),
        ],
        2 * images * PAD * (4 * width * width + 2 * PAD * width * 4),
        "decoder_attention",
    )


def dec_mlp_body(
    m_ref, ct_ref, vec_ref, up_ref, packed_ref,
    out_ref, dm_ref, grads_ref, gvec_ref,
    ct_s, up_s, down_s, vec_s, w_s, low_s, sems,
):
    step, last = pl.program_id(0), pl.num_programs(0) - 1
    count, rows, width = m_ref.shape
    hidden = up_ref.shape[1]
    blocks, block = packed_ref.shape[:2]
    groups = hidden // (blocks * block)
    columns = [slice(4 * width + hidden + k * width, 4 * width + hidden + (k + 1) * width) for k in range(groups)]
    parts = [slice(k * block, (k + 1) * block) for k in range(groups)]

    @pl.when(step == 0)
    def _():
        up_s[...] = jnp.zeros_like(up_s)
        down_s[...] = jnp.zeros_like(down_s)
        vec_s[...] = jnp.zeros_like(vec_s)
        ct_s[...] = jnp.zeros_like(ct_s)
        finish(begin([(packed_ref.at[:, :, columns[k]], w_s.at[:, parts[k]]) for k in range(groups)], sems))

    for j in range(count):
        ct_s[j, 0:PATCHES] = ct_ref[j].astype(jnp.float32)
    ct = ct_s[...].reshape(count * rows, width)
    d_out = low(ct)
    m = m_ref[...].reshape(count * rows, width)
    n2 = low(norm_apply(m, vec_ref[2:3], vec_ref[3:4]))
    y = m
    d_n2 = jnp.zeros_like(m)
    chunk = 512
    for at in range(0, hidden, chunk):
        up = up_ref[:, at : at + chunk]
        span = groups * block
        down = w_s[at // span : (at + chunk) // span].reshape(chunk, width)
        u = dot_nn(n2, up)
        phi, slope = gelu_parts(u)
        g = low(u * phi)
        y = y + dot_nn(g, down)
        d_u = low(dot_nt(d_out, down) * (phi + slope))
        d_n2 = d_n2 + dot_nt(d_u, up)
        down_s[at : at + chunk] += dot_tn(g, d_out)
        up_s[:, at : at + chunk] += dot_tn(n2, d_u)
    for j in range(count):
        out_ref[j] = low(y[j * rows : j * rows + PATCHES])
    d_m, g_gain, g_bias = norm_back(m, vec_ref[2:3], d_n2)
    dm_ref[...] = (ct + d_m).reshape(count, rows, width)
    vec_s[0:1] += g_gain
    vec_s[1:2] += g_bias

    @pl.when(step == last)
    def _():
        gvec_ref[...] = vec_s[...]
        w_s[...] = low(down_s[...]).reshape(w_s.shape)
        low_s[...] = low(up_s[...]).reshape(low_s.shape)
        pairs = [(w_s.at[:, parts[k]], grads_ref.at[:, :, columns[k]]) for k in range(groups)]
        pairs.append((low_s, grads_ref.at[:, :, slice(4 * width, 4 * width + hidden)]))
        finish(begin(pairs, sems))


def dec_mlp(m, cotangent, vec, packed):
    images, rows, width = m.shape
    blocks, block, columns = packed.shape
    hidden = (columns - 4 * width) // 2
    two = 2
    ins = [m, cotangent, vec, packed.reshape(blocks * block, columns), packed]
    outs = [b16(images, PATCHES, width), f32(images, rows, width), b16(blocks, block, columns), f32(8, width)]
    return call(
        dec_mlp_body,
        (images // two,),
        ins,
        [
            lead_spec(m.shape, two),
            lead_spec(cotangent.shape, two),
            full_spec(vec.shape),
            pl.BlockSpec((width, hidden), lambda i: (0, 4 * width // hidden)),
            ANY,
        ],
        outs,
        [lead_spec(outs[0].shape, two), lead_spec(outs[1].shape, two), ANY, full_spec(outs[3].shape)],
        [
            pltpu.VMEM((two, rows, width), jnp.float32),
            pltpu.VMEM((width, hidden), jnp.float32),
            pltpu.VMEM((hidden, width), jnp.float32),
            pltpu.VMEM((8, width), jnp.float32),
            pltpu.VMEM((blocks, hidden // blocks, width), jnp.bfloat16),
            pltpu.VMEM((blocks, block, hidden), jnp.bfloat16),
            pltpu.SemaphoreType.DMA((8,)),
        ],
        12 * images * rows * width * hidden,
        "decoder_mlp",
    )


def dec_back_body(
    key_ref, keycol_ref, vec_ref, wqkv_ref, wo_ref,
    dm_ref, z_ref, qkv_ref, o_ref, p_ref, il_ref, ot_ref, given_ref,
    de_ref, gvec_ref, grads_ref,
    low_s, sem, de_s, gqkv_s, gwo_s, vec_s, dov_s, dot_s, dos_s, kt_s, dqt_s, dqkv_s,
):
    step, last = pl.program_id(0), pl.num_programs(0) - 1
    count, rows, width = z_ref.shape
    heads = p_ref.shape[1]
    head = width // heads
    group = 128 // head
    scale = head ** (-0.5)

    @pl.when(step == 0)
    def _():
        de_s[...] = jnp.zeros_like(de_s)
        gqkv_s[...] = jnp.zeros_like(gqkv_s)
        gwo_s[...] = jnp.zeros_like(gwo_s)
        vec_s[...] = jnp.zeros_like(vec_s)

    dm = dm_ref[...].reshape(count * rows, width)
    dmb = low(dm)
    gwo_s[...] += dot_tn(o_ref[...].reshape(count * rows, width), dmb)
    dov_s[...] = dot_nt(dmb, wo_ref[...]).reshape(count, rows, width)

    def one_image(j, carry):
        dot_s[...] = dov_s[j].T
        for h in range(heads):
            at = slice(h * head, (h + 1) * head)
            dot_s[at] = dot_s[at] * il_ref[j, h : h + 1]
        dos_s[...] = low(dot_s[...].T)
        kt_s[...] = qkv_ref[j, :, width : 2 * width].T
        for quad in range(width // 128):
            lanes = slice(quad * 128, (quad + 1) * 128)
            queries = qkv_ref[j, :, quad * 128 : (quad + 1) * 128]
            values = qkv_ref[j, :, 2 * width + quad * 128 : 2 * width + (quad + 1) * 128]
            d_rows = dos_s[:, lanes]
            d_k = jnp.zeros((rows, 128), jnp.float32)
            d_v = jnp.zeros((rows, 128), jnp.float32)
            for slot in range(group):
                h = quad * group + slot
                at = slice(h * head, (h + 1) * head)
                d_head = dot_s[at]
                delta = jnp.sum(ot_ref[j, at].astype(jnp.float32) * d_head, axis=0, keepdims=True)
                p = p_ref[j, h]
                d_p = dot_nn(values, place_head(low(d_head), slot, group))
                d_s = low(p.astype(jnp.float32) * (d_p - delta))
                d_v = d_v + dot_nn(p, keep_lanes(d_rows, slot, head))
                d_k = d_k + dot_nn(d_s, keep_lanes(queries, slot, head))
                dqt_s[at] = dot_nn(kt_s[at], d_s)
            dqkv_s[j, :, width + quad * 128 : width + (quad + 1) * 128] = low(d_k * scale)
            dqkv_s[j, :, 2 * width + quad * 128 : 2 * width + (quad + 1) * 128] = low(d_v)
        dqkv_s[j, :, 0:width] = low(dqt_s[...].T * scale)
        return carry

    lax.fori_loop(0, count, one_image, 0)
    d_qkv = dqkv_s[...].reshape(count * rows, 3 * width)
    z = z_ref[...].reshape(count * rows, width)
    n1 = low(norm_apply(z, vec_ref[0:1], vec_ref[1:2]))
    gqkv_s[...] += dot_tn(n1, d_qkv)
    d_z, g_gain, g_bias = norm_back(z, vec_ref[0:1], dot_nt(d_qkv, wqkv_ref[...]))
    d_z = dm + d_z
    vec_s[0:1] += g_gain
    vec_s[1:2] += g_bias
    for j in range(count):
        d_one = d_z[j * rows : (j + 1) * rows]
        base = (step * count + j) * 256
        wanted = lax.broadcasted_iota(jnp.int32, (rows, 1), 0) + base
        seen = jnp.sum((key_ref[...] == wanted).astype(jnp.float32), axis=1, keepdims=True)
        vec_s[2:3] += jnp.sum((1.0 - seen) * d_one, axis=0, keepdims=True)
        wanted = lax.broadcasted_iota(jnp.int32, (1, rows), 1) + base
        match = low((keycol_ref[...] == wanted).astype(jnp.float32))
        de_s[...] += dot_nn(match, low(d_one))

    @pl.when(step == last)
    def _():
        de_ref[...] = low(de_s[...])
        gvec_ref[...] = vec_s[...]
        blocks, block = low_s.shape[:2]
        low_s[:, :, 0 : 3 * width] = low(gqkv_s[...]).reshape(blocks, block, 3 * width)
        low_s[:, :, 3 * width :] = low(gwo_s[...]).reshape(blocks, block, width)
        copy = pltpu.make_async_copy(low_s, grads_ref.at[:, :, 0 : 4 * width], sem)
        copy.start()
        copy.wait()


def dec_back(key, keycol, vec, packed, dm, z, qkv, o, p, il, ot, grads):
    images, rows, width = z.shape
    two = 2
    seq = key.shape[1]
    ins = [key, keycol, vec, packed, packed, dm, z, qkv, o, p, il, ot, grads]
    outs = [b16(seq, width), f32(8, width), b16(*grads.shape)]
    return call(
        dec_back_body,
        (images // two,),
        ins,
        [full_spec(x.shape) for x in ins[:3]]
        + [pl.BlockSpec((width, 3 * width), lambda i: (0, 0)), pl.BlockSpec((width, width), lambda i: (0, 3))]
        + [lead_spec(x.shape, two) for x in ins[5:12]]
        + [ANY],
        outs,
        [full_spec(x.shape) for x in outs[:2]] + [ANY],
        [
            pltpu.VMEM(grads.shape[:2] + (4 * width,), jnp.bfloat16),
            pltpu.SemaphoreType.DMA(()),
            pltpu.VMEM((seq, width), jnp.float32),
            pltpu.VMEM((width, 3 * width), jnp.float32),
            pltpu.VMEM((width, width), jnp.float32),
            pltpu.VMEM((8, width), jnp.float32),
            pltpu.VMEM((two, rows, width), jnp.float32),
            pltpu.VMEM((width, rows), jnp.float32),
            pltpu.VMEM((rows, width), jnp.bfloat16),
            pltpu.VMEM((width, rows), jnp.bfloat16),
            pltpu.VMEM((width, rows), jnp.float32),
            pltpu.VMEM((two, rows, 3 * width), jnp.bfloat16),
        ],
        2 * images * rows * (8 * width * width + 5 * rows * width * 4),
        "decoder_attention_back",
        {12: 2},
    )


def enc_attention_body(
    core_ref, own_ref, win_ref, segq_ref, segk_ref, mine_ref, other_ref,
    q_ref, kv_ref, o_ref, m_ref, p_ref, il_ref, ot_ref, vec_ref,
    wqkv_ref, wo_ref, cols_s, qt_s, vt_s, ot_s, bias_s, sems,
):
    step = pl.program_id(0)
    rows, width = m_ref.shape
    heads, keys = p_ref.shape[1], p_ref.shape[2]
    head = width // heads
    group = 128 // head
    kappa = head ** (-0.5) * LOG2E

    @pl.when(step == 0)
    def _():
        core = core_ref[0]
        pairs = []
        for half, ref in ((core, mine_ref), (1 - core, other_ref)):
            pairs += [
                (ref.at[:, 0 : 3 * width // 2], wqkv_ref.at[:, lanes_of(half, 3 * width // 2)]),
                (ref.at[:, 3 * width // 2 : 2 * width], wo_ref.at[:, lanes_of(half, width // 2)]),
                (ref.at[:, 2 * width : 2 * width + 128], cols_s.at[half]),
            ]
        finish(begin(pairs, sems))
        vec_ref[...] = cols_s[0].astype(jnp.float32).T[0:8]
        normed = low(norm_apply(win_ref[...].astype(jnp.float32), vec_ref[0:1], vec_ref[1:2]))
        kv_ref[...] = low(dot_nn(normed, wqkv_ref[:, width:]))

    x = own_ref[...].astype(jnp.float32)
    normed = low(norm_apply(x, vec_ref[0:1], vec_ref[1:2]))
    q_ref[...] = low(dot_nn(normed, wqkv_ref[:, 0:width]))
    qt_s[...] = q_ref[...].T
    window = pl.ds(pl.multiple_of(step * 128, 128), keys)
    vt_s[...] = kv_ref[window, width:].T
    bias_s[...] = jnp.where(segk_ref[window, :] == segq_ref[...], 0.0, NEGATIVE)
    for h in range(heads):
        pair, slot = divmod(h, group)
        at = slice(h * head, (h + 1) * head)
        keys_pair = kv_ref[window, 128 * pair : 128 * (pair + 1)]
        s = dot_nn(keys_pair, place_head(qt_s[at], slot, group)) + bias_s[...]
        p = jnp.exp2((s - jnp.max(s, axis=0, keepdims=True)) * kappa)
        inverse = 1.0 / jnp.sum(p, axis=0, keepdims=True)
        p = low(p)
        p_ref[0, h] = p
        il_ref[0, h : h + 1] = inverse
        ot_s[at] = dot_nn(vt_s[at], p) * inverse
    ot_ref[0] = low(ot_s[...])
    o_ref[...] = low(ot_s[...].T)
    m_ref[...] = x + dot_nn(o_ref[...], wo_ref[...])


def enc_attention(core, own, window, seg_own, seg_window, mine, other):
    rows, width = own.shape
    total = window.shape[0]
    half = rows // 2
    keys = total - 128
    ins = [core, own, window, seg_own, seg_window, mine, other]
    in_specs = [
        SMEM,
        lead_spec(own.shape, half),
        full_spec(window.shape),
        pl.BlockSpec((1, half), lambda i: (0, i)),
        full_spec(seg_window.shape),
        ANY,
        ANY,
    ]
    outs = [
        b16(rows, width),
        b16(total, 2 * width),
        b16(rows, width),
        f32(rows, width),
        b16(2, HEADS, keys, half),
        f32(2, 16, half),
        b16(2, width, half),
        f32(8, width),
    ]
    out_specs = (
        [
            lead_spec(outs[0].shape, half),
            full_spec(outs[1].shape),
            lead_spec(outs[2].shape, half),
            lead_spec(outs[3].shape, half),
        ]
        + [lead_spec(x.shape, 1) for x in outs[4:7]]
        + [full_spec(outs[7].shape)]
    )
    return call(
        enc_attention_body,
        (2,),
        ins,
        in_specs,
        outs,
        out_specs,
        [
            pltpu.VMEM((width, 3 * width), jnp.bfloat16),
            pltpu.VMEM((width, width), jnp.bfloat16),
            pltpu.VMEM((2, width, 128), jnp.bfloat16),
            pltpu.VMEM((width, half), jnp.bfloat16),
            pltpu.VMEM((width, keys), jnp.bfloat16),
            pltpu.VMEM((width, half), jnp.float32),
            pltpu.VMEM((keys, half), jnp.float32),
            pltpu.SemaphoreType.DMA((6,)),
        ],
        2 * rows * (4 * width * width + 4 * keys * width),
        "encoder_attention",
    )


CHUNK = 768


def mlp_weights(core, mine_up, other_up, mine_down, other_down, up_s, down_s, embed_s):
    half_up = up_s.shape[2] // 2
    half_down = down_s.shape[2] // 2
    block = mine_down.shape[1]
    ups, embeds, downs = [], [], []
    for half, up, down in ((core, mine_up, mine_down), (1 - core, other_up, other_down)):
        ups.append((up.at[:, :, 0:half_up], up_s.at[:, :, lanes_of(half, half_up)]))
        for k, ref in enumerate((up, down)):
            lanes = pl.ds(pl.multiple_of(half * 256 + k * 128, 128), 128)
            embeds.append((ref.at[:, :, half_up : half_up + 128], embed_s.at[:, :, lanes]))
        for k in range(down_s.shape[1] // block):
            downs.append(
                (
                    down.at[:, :, k * half_down : (k + 1) * half_down],
                    down_s.at[:, k * block : (k + 1) * block, lanes_of(half, half_down)],
                )
            )
    return ups, embeds, downs


def enc_mlp_body(
    core_ref, m_ref, vec_ref, mu_ref, ou_ref, md_ref, od_ref,
    g_ref, slope_ref, h_ref, e_ref,
    up_s, down_s, embed_s, n2_s, y_s, sems,
):
    step, last = pl.program_id(0), pl.num_programs(0) - 1
    width = m_ref.shape[1]
    ups, embeds, downs = mlp_weights(core_ref[0], mu_ref, ou_ref, md_ref, od_ref, up_s, down_s, embed_s)

    @pl.when(step == 0)
    def _():
        up_copies = begin(ups, sems)
        rest = begin(downs + embeds, sems, len(ups))
        m = m_ref[...]
        n2_s[...] = low(norm_apply(m, vec_ref[2:3], vec_ref[3:4]))
        y_s[...] = m
        finish(up_copies + rest)

    up = up_s[:, :, pl.ds(pl.multiple_of(step * CHUNK, CHUNK), CHUNK)].reshape(width, CHUNK)
    span = CHUNK // down_s.shape[1]
    down = down_s[pl.ds(step * span, span)].reshape(CHUNK, width)
    u = dot_nn(n2_s[...], up)
    phi, slope = gelu_parts(u)
    g = low(u * phi)
    g_ref[...] = g
    slope_ref[...] = low(phi + slope)
    y_s[...] += dot_nn(g, down)

    @pl.when(step == last)
    def _():
        h = low(y_s[...])
        h_ref[...] = h
        e_ref[...] = low(dot_nn(h, embed_s[...].reshape(width, embed_s.shape[2])))


def mlp_scratch(blocks, block, width, hidden, embed):
    return [
        pltpu.VMEM((blocks, block, hidden), jnp.bfloat16),
        pltpu.VMEM((blocks, hidden // blocks, width), jnp.bfloat16),
        pltpu.VMEM((blocks, block, embed), jnp.bfloat16),
    ]


def enc_mlp(core, m, vec, mine_up, other_up, mine_down, other_down, hidden):
    rows, width = m.shape
    blocks, block = mine_up.shape[:2]
    embed = DD
    ins = [core, m, vec, mine_up, other_up, mine_down, other_down]
    outs = [b16(rows, hidden), b16(rows, hidden), b16(rows, width), b16(rows, embed)]
    columns = pl.BlockSpec((rows, CHUNK), lambda i: (0, i))
    return call(
        enc_mlp_body,
        (hidden // CHUNK,),
        ins,
        [SMEM, full_spec(m.shape), full_spec(vec.shape), ANY, ANY, ANY, ANY],
        outs,
        [columns, columns, full_spec(outs[2].shape), full_spec(outs[3].shape)],
        mlp_scratch(blocks, block, width, hidden, embed)
        + [
            pltpu.VMEM((rows, width), jnp.bfloat16),
            pltpu.VMEM((rows, width), jnp.float32),
            pltpu.SemaphoreType.DMA((16,)),
        ],
        4 * rows * width * hidden,
        "encoder_mlp",
    )


def enc_mlp_back_body(
    core_ref, de_ref, h_ref, m_ref, vec_ref, g_ref, slope_ref, mu_ref, ou_ref, md_ref, od_ref,
    umine_ref, uother_ref, dmine_ref, dother_ref, dm_ref, gvec_ref,
    up_s, down_s, embed_s, gup_s, gdown_s, n2t_s, dy_s, dyb_s, dn2_s, sems, out_sems,
):
    step, last = pl.program_id(0), pl.num_programs(0) - 1
    width = m_ref.shape[1]
    embed = embed_s.shape[2]
    core = core_ref[0]
    ups, embeds, downs = mlp_weights(core, mu_ref, ou_ref, md_ref, od_ref, up_s, down_s, embed_s)

    @pl.when(step == 0)
    def _():
        first = begin(embeds, sems)
        rest = begin(downs + ups, sems, len(embeds))
        n2t_s[...] = low(norm_apply(m_ref[...], vec_ref[2:3], vec_ref[3:4])).T
        dn2_s[...] = jnp.zeros_like(dn2_s)
        finish(first)
        d_y = dot_nt(de_ref[...], embed_s[...].reshape(width, embed))
        dy_s[...] = d_y
        dyb_s[...] = low(d_y)
        embed_s[...] = low(dot_tn(h_ref[...], de_ref[...])).reshape(embed_s.shape)
        finish(rest)

    columns = pl.ds(pl.multiple_of(step * CHUNK, CHUNK), CHUNK)
    span = CHUNK // down_s.shape[1]
    groups = pl.ds(step * span, span)
    up = up_s[:, :, columns].reshape(width, CHUNK)
    down = down_s[groups].reshape(CHUNK, width)
    d_out = dyb_s[...]
    d_u = low(dot_nt(d_out, down) * slope_ref[...].astype(jnp.float32))
    gdown_s[groups] = low(dot_tn(g_ref[...], d_out)).reshape(span, down_s.shape[1], width)
    gup_s[:, :, columns] = low(dot_nn(n2t_s[...], d_u)).reshape(up_s.shape[0], up_s.shape[1], CHUNK)
    dn2_s[...] += dot_nt(d_u, up)

    @pl.when(step == last)
    def _():
        sent = mlp_weights(core, umine_ref, uother_ref, dmine_ref, dother_ref, gup_s, gdown_s, embed_s)
        copies = begin([(target, source) for source, target in sent[0] + sent[1] + sent[2]], out_sems)
        d_m, g_gain, g_bias = norm_back(m_ref[...], vec_ref[2:3], dn2_s[...])
        dm_ref[...] = dy_s[...] + d_m
        gvec_ref[...] = jnp.concatenate(
            [g_gain, g_bias, jnp.zeros((6, g_gain.shape[1]), jnp.float32)], axis=0
        )
        finish(copies)


def enc_mlp_back(core, de, h, m, vec, g, slope, mine_up, other_up, mine_down, other_down):
    rows, width = m.shape
    hidden = g.shape[1]
    blocks, block, columns = mine_up.shape
    embed = de.shape[1]
    ins = [core, de, h, m, vec, g, slope, mine_up, other_up, mine_down, other_down]
    spec = pl.BlockSpec((rows, CHUNK), lambda i: (0, i))
    outs = [b16(blocks, block, columns)] * 4 + [f32(rows, width), f32(8, width)]
    scratch = mlp_scratch(blocks, block, width, hidden, embed)
    return call(
        enc_mlp_back_body,
        (hidden // CHUNK,),
        ins,
        [SMEM] + [full_spec(x.shape) for x in ins[1:5]] + [spec, spec, ANY, ANY, ANY, ANY],
        outs,
        [ANY] * 4 + [full_spec(x.shape) for x in outs[4:]],
        scratch
        + scratch[:2]
        + [
            pltpu.VMEM((width, rows), jnp.bfloat16),
            pltpu.VMEM((rows, width), jnp.float32),
            pltpu.VMEM((rows, width), jnp.bfloat16),
            pltpu.VMEM((rows, width), jnp.float32),
            pltpu.SemaphoreType.DMA((16,)),
            pltpu.SemaphoreType.DMA((16,)),
        ],
        8 * rows * width * hidden,
        "encoder_mlp_back",
    )


def enc_attention_back_body(
    core_ref, dm_ref, q_ref, kv_ref, p_ref, il_ref, ot_ref, mine_ref, other_ref,
    dq_ref, dkv_ref,
    wo_ref, dot_s, dos_s, kt_s, dqt_s, sems,
):
    step = pl.program_id(0)
    rows, width = dm_ref.shape
    heads, keys = p_ref.shape[1], p_ref.shape[2]
    head = width // heads
    group = 128 // head
    scale = head ** (-0.5)

    @pl.when(step == 0)
    def _():
        pairs = [
            (ref.at[:, 3 * width // 2 : 2 * width], wo_ref.at[:, lanes_of(half, width // 2)])
            for half, ref in ((core_ref[0], mine_ref), (1 - core_ref[0], other_ref))
        ]
        copies = begin(pairs, sems)
        dkv_ref[...] = jnp.zeros_like(dkv_ref)
        finish(copies)

    dmb = low(dm_ref[...])
    dot_s[...] = dot_nt(dmb, wo_ref[...]).T
    for h in range(heads):
        at = slice(h * head, (h + 1) * head)
        dot_s[at] = dot_s[at] * il_ref[0, h : h + 1]
    dos_s[...] = low(dot_s[...].T)
    window = pl.ds(pl.multiple_of(step * 128, 128), keys)
    kt_s[...] = kv_ref[window, 0:width].T
    for pair in range(width // 128):
        lanes = slice(pair * 128, (pair + 1) * 128)
        queries = q_ref[:, lanes]
        values = kv_ref[window, width + pair * 128 : width + (pair + 1) * 128]
        d_rows = dos_s[:, lanes]
        d_k = jnp.zeros((keys, 128), jnp.float32)
        d_v = jnp.zeros((keys, 128), jnp.float32)
        for slot in range(group):
            h = pair * group + slot
            at = slice(h * head, (h + 1) * head)
            d_head = dot_s[at]
            delta = jnp.sum(ot_ref[0, at].astype(jnp.float32) * d_head, axis=0, keepdims=True)
            p = p_ref[0, h]
            d_p = dot_nn(values, place_head(low(d_head), slot, group))
            d_s = low(p.astype(jnp.float32) * (d_p - delta))
            d_v = d_v + dot_nn(p, keep_lanes(d_rows, slot, head))
            d_k = d_k + dot_nn(d_s, keep_lanes(queries, slot, head))
            dqt_s[at] = dot_nn(kt_s[at], d_s)
        dkv_ref[window, pair * 128 : (pair + 1) * 128] += d_k * scale
        dkv_ref[window, width + pair * 128 : width + (pair + 1) * 128] += d_v
    dq_ref[...] = low(dqt_s[...].T * scale)


def enc_attention_back(core, dm, q, kv, p, il, ot, mine, other):
    rows, width = dm.shape
    total = kv.shape[0]
    half = rows // 2
    keys = total - 128
    ins = [core, dm, q, kv, p, il, ot, mine, other]
    block = lead_spec(dm.shape, half)
    outs = [b16(rows, width), f32(total, 2 * width)]
    return call(
        enc_attention_back_body,
        (2,),
        ins,
        [SMEM, block, block, full_spec(kv.shape)] + [lead_spec(x.shape, 1) for x in ins[4:7]] + [ANY, ANY],
        outs,
        [block, full_spec(outs[1].shape)],
        [
            pltpu.VMEM((width, width), jnp.bfloat16),
            pltpu.VMEM((width, half), jnp.float32),
            pltpu.VMEM((half, width), jnp.bfloat16),
            pltpu.VMEM((width, keys), jnp.bfloat16),
            pltpu.VMEM((width, half), jnp.float32),
            pltpu.SemaphoreType.DMA((2,)),
        ],
        2 * rows * (width * width + 10 * keys * width),
        "encoder_attention_back",
    )


def enc_qkv_back_body(
    core_ref, own_ref, dm_ref, o_ref, dq_ref, dkv_ref, got_ref, vec_ref, gvec2_ref, dvec_ref,
    mine_ref, other_ref,
    gmine_ref, gother_ref, dr_ref,
    wqkv_s, gqkv_s, gwo_s, cols_s, dqkv_s, sems, out_sems,
):
    rows, width = dm_ref.shape
    near = got_ref.shape[0]
    core = core_ref[0]
    halves_at = ((core, mine_ref, gmine_ref), (1 - core, other_ref, gother_ref))
    weights = begin(
        [
            (ref.at[:, 0 : 3 * width // 2], wqkv_s.at[:, lanes_of(half, 3 * width // 2)])
            for half, ref, _ in halves_at
        ],
        sems,
    )
    x = own_ref[...].astype(jnp.float32)
    n1t = low(norm_apply(x, vec_ref[0:1], vec_ref[1:2])).T
    gwo_s[...] = low(dot_tn(o_ref[...], low(dm_ref[...])))
    sent = begin(
        [
            (gwo_s.at[:, lanes_of(half, width // 2)], ref.at[:, 3 * width // 2 : 2 * width])
            for half, _, ref in halves_at
        ],
        out_sems,
    )
    dqkv_s[0] = dq_ref[...]
    first = pl.ds(pl.multiple_of(core * near, near), rows)
    edge = pl.ds(pl.multiple_of((1 - core) * (rows - near), near), near)
    edge_in = pl.ds(pl.multiple_of(core * near + (1 - core) * (rows - near), near), near)
    for k in range(2):
        lanes = slice(k * width, (k + 1) * width)
        dqkv_s[k + 1] = low(dkv_ref[first, lanes])
        dqkv_s[k + 1, edge] = low(dkv_ref[edge_in, lanes] + got_ref[:, lanes].astype(jnp.float32))
    finish(weights)
    d_n1 = jnp.zeros((rows, width), jnp.float32)
    for k in range(3):
        lanes = slice(k * width, (k + 1) * width)
        d_part = dqkv_s[k]
        gqkv_s[:, lanes] = low(dot_nn(n1t, d_part))
        d_n1 = d_n1 + dot_nt(d_part, wqkv_s[:, lanes])
    sent += begin(
        [
            (gqkv_s.at[:, lanes_of(half, 3 * width // 2)], ref.at[:, 0 : 3 * width // 2])
            for half, _, ref in halves_at
        ],
        out_sems,
        2,
    )
    d_r, g_gain, g_bias = norm_back(x, vec_ref[0:1], d_n1)
    dr_ref[...] = dm_ref[...] + d_r
    grads = jnp.concatenate(
        [g_gain, g_bias, gvec2_ref[0:2], jnp.zeros((124, width), jnp.float32)], axis=0
    )
    cols_s[0] = low(grads.T)
    cols_s[1] = dvec_ref[...]
    sent += begin(
        [(cols_s.at[half], ref.at[:, 2 * width : 2 * width + 128]) for half, _, ref in halves_at],
        out_sems,
        4,
    )
    finish(sent)


def enc_qkv_back(core, own, dm, o, dq, dkv, got, vec, gvec2, dvec, mine, other):
    rows, width = dm.shape
    ins = [core, own, dm, o, dq, dkv, got, vec, gvec2, dvec, mine, other]
    outs = [b16(*mine.shape), b16(*mine.shape), f32(rows, width)]
    return call(
        enc_qkv_back_body,
        (1,),
        ins,
        [SMEM] + [full_spec(x.shape) for x in ins[1:10]] + [ANY, ANY],
        outs,
        [ANY, ANY, full_spec(outs[2].shape)],
        [
            pltpu.VMEM((width, 3 * width), jnp.bfloat16),
            pltpu.VMEM((width, 3 * width), jnp.bfloat16),
            pltpu.VMEM((width, width), jnp.bfloat16),
            pltpu.VMEM((2, width, 128), jnp.bfloat16),
            pltpu.VMEM((3, rows, width), jnp.bfloat16),
            pltpu.SemaphoreType.DMA((2,)),
            pltpu.SemaphoreType.DMA((6,)),
        ],
        14 * rows * width * width,
        "encoder_qkv_back",
    )


def shards(
    inputs,
    enc_norm_gain,
    enc_norm_bias,
    enc_qkv,
    enc_proj,
    enc_mlp_gain,
    enc_mlp_bias,
    enc_up,
    enc_down,
    embed_weight,
    mask_token,
    dec_norm_gain,
    dec_norm_bias,
    dec_qkv,
    dec_proj,
    dec_mlp_gain,
    dec_mlp_bias,
    dec_up,
    dec_down,
    cotangent,
    visible_counts,
    patch_positions,
    image_owner,
):
    core = lax.axis_index("narrow").astype(jnp.int32)
    wide_index = lax.axis_index("wide")
    cores = lax.axis_size("narrow")
    grid = Grid(lax.axis_size("wide"))
    devices = grid.wide * cores
    half_rows = inputs.shape[1]
    slot_count = IMG_SEQ // cores
    rows_e, rows_d = enc_qkv.shape[0], dec_qkv.shape[0]
    width_e, width_d = enc_proj.shape[1], dec_proj.shape[1]
    wide_e, wide_d = enc_up.shape[1], dec_up.shape[1]
    half_q, half_p, half_u, half_v = 3 * width_e // 2, width_e // 2, wide_e // 2, width_d // 2

    vectors_e = jnp.stack([enc_norm_gain, enc_norm_bias, enc_mlp_gain, enc_mlp_bias], axis=1)
    vectors_d = jnp.stack(
        [dec_norm_gain, dec_norm_bias, dec_mlp_gain, dec_mlp_bias, mask_token], axis=1
    )
    packs = []
    for half, vectors in enumerate((vectors_e, vectors_d)):
        vectors = jnp.pad(vectors, ((0, rows_e - vectors.shape[0]), (0, 128 - vectors.shape[1])))
        packs.append(
            jnp.concatenate(
                [
                    enc_qkv[:, half * half_q : (half + 1) * half_q],
                    enc_proj[:, half * half_p : (half + 1) * half_p],
                    vectors,
                    enc_up[:, half * half_u : (half + 1) * half_u],
                    embed_weight[:, half * half_v : (half + 1) * half_v],
                ],
                axis=1,
            )
        )
    own_pack = jnp.where(core == 0, packs[0], packs[1])
    other_pack = jnp.where(core == 0, packs[1], packs[0])
    chip_pack = in_order(own_pack, lax.ppermute(other_pack, "narrow", SWAP), core, 0)
    chip_down = chip_rows(enc_down, core)
    chip_block = cores * rows_e
    down_groups = chip_down.shape[0] // chip_block
    part = half_q + half_p + 128
    parts = [
        chip_pack[:, :part],
        chip_pack[:, part : 2 * part],
        jnp.concatenate(
            [chip_down[k * chip_block : (k + 1) * chip_block] for k in range(down_groups)]
            + [chip_pack[:, 2 * part :]],
            axis=1,
        ),
    ]
    group_d = dec_down.shape[0] // rows_d
    dec_packed = jnp.concatenate(
        [dec_qkv, dec_proj, dec_up] + [dec_down[k * rows_d : (k + 1) * rows_d] for k in range(group_d)],
        axis=1,
    )
    dec_whole = lax.all_gather(dec_packed, ("wide", "narrow"), axis=0, tiled=True)
    dec_whole = regroup(
        dec_whole.reshape(devices, rows_d, dec_whole.shape[1]), DEC_BLOCK, 4 * width_d + wide_d, width_d
    )

    def full_parts(gathered):
        shaped = [gathered[k].reshape(-1, ENC_BLOCK, part) for k in range(2)]
        return shaped + [regroup(gathered[2], ENC_BLOCK, 0, half_p, down_groups)]

    wide_parts = gather_parts(grid, parts)
    mine = full_parts(wide_parts)
    other = full_parts([lax.ppermute(w, "narrow", SWAP) for w in wide_parts])
    mine_first, other_first = [x.reshape(width_e, part) for x in (mine[0], other[0])]
    vectors_two = jnp.where(core == 0, other_first[:, -128:], mine_first[:, -128:])
    vectors_two = vectors_two.reshape(devices, rows_e, 128)[:, :rows_d].reshape(width_d, 128)
    dec_rows = vectors_two.astype(jnp.float32).T[:8]

    image_ends = jnp.cumsum(visible_counts[0], axis=0)
    position = jnp.arange(SEQ, dtype=jnp.int32)
    segment_all = jnp.sum((image_ends[None, :] <= position[:, None]).astype(jnp.int32), axis=1)
    segment_own = lax.dynamic_slice_in_dim(segment_all, core * half_rows, half_rows, 0)
    other_positions = lax.ppermute(patch_positions[0], "narrow", SWAP)
    sequence_positions = in_order(patch_positions[0], other_positions, core, 0)
    owners = lax.dynamic_slice_in_dim(image_owner, wide_index * IMG_SEQ, IMG_SEQ, 0)
    local_slot = owners - (wide_index * cores + core) * slot_count
    slot_base = jnp.where((local_slot >= 0) & (local_slot < slot_count), local_slot * 256, -256)
    row_base = jnp.sum(
        jnp.where(segment_all[:, None] == jnp.arange(IMG_SEQ)[None, :], slot_base[None, :], 0), axis=1
    )
    key = jnp.where(row_base >= 0, row_base + sequence_positions, -1).astype(jnp.int32)
    posn = jnp.pad(position_table(width_d), ((0, PAD - PATCHES), (0, 0)))

    near = 128
    own_rows = inputs[0]
    edge = lax.dynamic_slice_in_dim(own_rows, (1 - core) * (half_rows - near), near, 0)
    window_rows = in_order(own_rows, lax.ppermute(edge, "narrow", SWAP), core, 0)
    seg_window = lax.dynamic_slice_in_dim(segment_all, core * (half_rows - near), half_rows + near, 0)
    core_one = core[None]
    queries, keys_values, context, middle, probs, inverse, context_t, enc_rows = enc_attention(
        core_one, own_rows, window_rows, segment_own[None, :], seg_window[:, None], mine_first, other_first
    )
    hidden_act, hidden_slope, encoded_low, embedded = enc_mlp(
        core_one, middle, enc_rows, mine[1], other[1], mine[2], other[2], wide_e
    )

    sequence_embedded = in_order(embedded, lax.ppermute(embedded, "narrow", SWAP), core, 0)
    dec_flat = dec_whole.reshape(width_d, dec_whole.shape[2])
    z, packed_d, context_d, middle_d, probs_d, inverse_d, context_td = dec_attention(
        key[None, :], sequence_embedded, posn, dec_rows, dec_flat, slot_count
    )
    decoded, d_middle_d, grads_d, grad_dec_vec2 = dec_mlp(middle_d, cotangent, dec_rows, dec_whole)
    d_sequence, grad_dec_vec1, grads_d = dec_back(
        key[None, :], key[:, None], dec_rows, dec_flat,
        d_middle_d, z, packed_d, context_d, probs_d, inverse_d, context_td, grads_d,
    )
    grads_d = regroup(grads_d, rows_d, 4 * width_d + wide_d, width_d)
    sum_d = lax.psum_scatter(
        grads_d.reshape(width_d, -1), ("wide", "narrow"), scatter_dimension=0, tiled=True
    )

    d_mine = lax.dynamic_slice_in_dim(d_sequence, core * half_rows, half_rows, 0)
    d_theirs = lax.dynamic_slice_in_dim(d_sequence, (1 - core) * half_rows, half_rows, 0)
    d_embedded = low(
        d_mine.astype(jnp.float32) + lax.ppermute(d_theirs, "narrow", SWAP).astype(jnp.float32)
    )
    up_mine, up_other, down_mine, down_other, d_middle, grad_vec2 = enc_mlp_back(
        core_one, d_embedded, encoded_low, middle, enc_rows, hidden_act, hidden_slope,
        mine[1], other[1], mine[2], other[2],
    )

    def summed(own, theirs, order):
        got = lax.ppermute(theirs, "narrow", SWAP)
        return scatter_part(grid, [own, got], order)

    sum_up = summed(up_mine, up_other, (2, 1, 0))
    sum_down = summed(
        *[regroup(x, chip_block, 0, half_p, down_groups) for x in (down_mine, down_other)], (1, 2, 0)
    )
    d_queries, d_keys_values = enc_attention_back(
        core_one, d_middle, queries, keys_values, probs, inverse, context_t, mine_first, other_first
    )
    d_far = lax.dynamic_slice_in_dim(d_keys_values, (1 - core) * half_rows, near, 0)
    d_got = lax.ppermute(low(d_far), "narrow", SWAP)
    columns_d = jnp.stack(
        [grad_dec_vec1[0], grad_dec_vec1[1], grad_dec_vec2[0], grad_dec_vec2[1], grad_dec_vec1[2]], axis=1
    )
    columns_d = jnp.pad(
        low(columns_d).reshape(devices, rows_d, 5), ((0, 0), (0, rows_e - rows_d), (0, 123))
    ).reshape(width_e, 128)
    first_mine, first_other, d_inputs = enc_qkv_back(
        core_one, own_rows, d_middle, context, d_queries, d_keys_values, d_got,
        enc_rows, grad_vec2, columns_d, mine_first, other_first,
    )
    cut = 896
    sum_first = jnp.concatenate(
        [
            summed(first_mine[:, :cut], first_other[:, :cut], (2, 1, 0)),
            summed(first_mine[:, cut:], first_other[:, cut:], (1, 2, 0)),
        ],
        axis=1,
    )

    groups = [sum_down[:, k * half_p : (k + 1) * half_p] for k in range(down_groups)]
    row_pack = jnp.concatenate([sum_first, sum_up, sum_down[:, down_groups * half_p :]], axis=1)
    out_down = core_rows(jnp.concatenate(groups, axis=0), core)
    own_out = lax.dynamic_slice_in_dim(row_pack, core * rows_e, rows_e, 0)
    send_out = lax.dynamic_slice_in_dim(row_pack, (1 - core) * rows_e, rows_e, 0)
    got_out = lax.ppermute(send_out, "narrow", SWAP)
    halves_out = [jnp.where(core == 0, own_out, got_out), jnp.where(core == 0, got_out, own_out)]

    def columns(start, count):
        return jnp.concatenate([x[:, start : start + count] for x in halves_out], axis=1)

    vec_e = halves_out[0][:, half_q + half_p : part]
    vec_d = halves_out[1][:rows_d, half_q + half_p : part]
    sum_d = sum_d.astype(jnp.float32)
    at_d = 4 * width_d + wide_d
    return (
        decoded,
        d_inputs.reshape(inputs.shape),
        vec_e[:, 0],
        vec_e[:, 1],
        columns(0, half_q),
        columns(half_q, half_p),
        vec_e[:, 2],
        vec_e[:, 3],
        columns(part, half_u),
        out_down,
        columns(part + half_u, half_v),
        vec_d[:, 4],
        vec_d[:, 0],
        vec_d[:, 1],
        sum_d[:, : 3 * width_d],
        sum_d[:, 3 * width_d : 4 * width_d],
        vec_d[:, 2],
        vec_d[:, 3],
        sum_d[:, 4 * width_d : at_d],
        jnp.concatenate(
            [sum_d[:, at_d + k * width_d : at_d + (k + 1) * width_d] for k in range(group_d)], axis=0
        ),
    )


def solution(mesh):
    in_specs = (
        P("wide", "narrow", None),
        P(("wide", "narrow")),
        P(("wide", "narrow")),
        P(("wide", "narrow"), None),
        P(("wide", "narrow"), None),
        P(("wide", "narrow")),
        P(("wide", "narrow")),
        P(("wide", "narrow"), None),
        P(("wide", "narrow"), None),
        P(("wide", "narrow"), None),
        P(("wide", "narrow")),
        P(("wide", "narrow")),
        P(("wide", "narrow")),
        P(("wide", "narrow"), None),
        P(("wide", "narrow"), None),
        P(("wide", "narrow")),
        P(("wide", "narrow")),
        P(("wide", "narrow"), None),
        P(("wide", "narrow"), None),
        P(("wide", "narrow"), None, None),
        P("wide", None),
        P("wide", "narrow"),
        P(),
    )
    out_specs = (
        P(("wide", "narrow"), None, None),
        P("wide", "narrow", None),
        P(("wide", "narrow")),
        P(("wide", "narrow")),
        P(("wide", "narrow"), None),
        P(("wide", "narrow"), None),
        P(("wide", "narrow")),
        P(("wide", "narrow")),
        P(("wide", "narrow"), None),
        P(("wide", "narrow"), None),
        P(("wide", "narrow"), None),
        P(("wide", "narrow")),
        P(("wide", "narrow")),
        P(("wide", "narrow")),
        P(("wide", "narrow"), None),
        P(("wide", "narrow"), None),
        P(("wide", "narrow")),
        P(("wide", "narrow")),
        P(("wide", "narrow"), None),
        P(("wide", "narrow"), None),
    )
    return jax.shard_map(shards, mesh=mesh, in_specs=in_specs, out_specs=out_specs, check_vma=False)
```
